512 devices in a mesh: wave: 8 (over y_hi, x), tile: 64 (over z, y_lo, core).
Axes of the slice: x: 4, y: 8 (y_hi: 2, y_lo: 4; y = y_hi * 4 + y_lo), z: 8, core: 2. Of those that a mesh axis runs over, the one named last changes fastest.
Arguments:
- e_forward: float32 [8, 3, 1024, 16, 128], P('wave', None, 'tile'), may hold values from -6 to 6
- h_forward: float32 [8, 3, 1024, 16, 128], P('wave', None, 'tile'), may hold values from -6 to 6
- e_adjoint: float32 [8, 3, 1024, 16, 128], P('wave', None, 'tile'), may hold values from -6 to 6
- h_adjoint: float32 [8, 3, 1024, 16, 128], P('wave', None, 'tile'), may hold values from -6 to 6
- eps_table: float32 [8, 4], P('wave'), may hold values from 1 to 6
- material: int32 [1024, 16, 128], P('tile'), may hold values from 0 to 3
- pml_depth: int32 [1024, 16, 128], P('tile'), may hold values from 0 to 4
- design_start: int32 [64], P('tile'), may hold values from 0 to 112
Outputs:
- e_forward_out: float32 [8, 3, 1024, 16, 128], P('wave', None, 'tile')
- h_forward_out: float32 [8, 3, 1024, 16, 128], P('wave', None, 'tile')
- e_adjoint_out: float32 [8, 3, 1024, 16, 128], P('wave', None, 'tile')
- h_adjoint_out: float32 [8, 3, 1024, 16, 128], P('wave', None, 'tile')
- gradient: float32 [1024, 16, 16], P('tile')
The draws below stay inside these ranges and needn't reach their ends.
All inputs are finite; a program needn't handle non-finite values.
Results may differ from the reference program's by a relative error of at most 0.0003.
Values sent between devices are 32-bit elements; how exact they have to be, the bound alone decides.
No kernel may reach another device: no remote copies, remote signals or barrier semaphores. Data moves between devices by JAX's collectives and lax.ppermute only.
A program may use at most 64 MiB of HBM per device.

```python
import jax
import jax.numpy as jnp
from jax import lax

CX = 16
CY = 16
CZ = 128
STEPS = 4
DZ = 16
NMAT = 4
TILE_COLS = 8
WAVES = 8
ROWS = 1024
N_WAVE = 8
N_TILE = 64


def place_ends(array, own_key, smallest, largest):
    index_at = [jax.random.randint(jax.random.fold_in(own_key, axis), (), 0, length) for axis, length in enumerate(array.shape)]
    widest = array.shape.index(max(array.shape))
    beside = index_at[:widest] + [(index_at[widest] + 1) % array.shape[widest]] + index_at[widest + 1:]
    return array.at[tuple(index_at)].set(smallest).at[tuple(beside)].set(largest)


def level_of(key, dims, cuts, smallest, high):
    level, own = 1.0, jax.random.fold_in(key, 6)
    for position, parts in cuts:
        heights = jnp.exp(jax.random.uniform(jax.random.fold_in(own, position), (parts,), jnp.float32, smallest / len(cuts), high / len(cuts)))
        level = level * jnp.repeat(heights, dims[position] // parts).reshape([-1 if axis == position else 1 for axis in range(len(dims))])
    return level


def noise(rng, shape, deviation, most, split=(), kind=jnp.bfloat16):
    entries = deviation * jax.random.normal(rng, shape, jnp.float32)
    if split:
        entries = entries * level_of(rng, shape, split, -0.22, 0.18)
    return jnp.clip(entries, -most, most).astype(kind)


def setup_inputs(seed: int = 0) -> dict:
    arg_keys = jax.random.split(jax.random.key(seed), 9)
    return {
        "e_forward": noise(arg_keys[0], (WAVES, 3, ROWS, CY, CZ), 1.0, 6.0, ((0, 8), (2, 64)), jnp.float32),
        "h_forward": noise(arg_keys[1], (WAVES, 3, ROWS, CY, CZ), 1.0, 6.0, ((0, 8), (2, 64)), jnp.float32),
        "e_adjoint": noise(arg_keys[2], (WAVES, 3, ROWS, CY, CZ), 1.0, 6.0, ((0, 8), (2, 64)), jnp.float32),
        "h_adjoint": noise(arg_keys[3], (WAVES, 3, ROWS, CY, CZ), 1.0, 6.0, ((0, 8), (2, 64)), jnp.float32),
        "eps_table": jnp.clip(1.0 + 5.0 * jax.random.uniform(arg_keys[4], (WAVES, NMAT), jnp.float32) ** level_of(arg_keys[4], (WAVES, NMAT), ((0, 8),), -0.2, 0.2), 1.0, 6.0),
        "material": place_ends(jax.random.randint(arg_keys[5], (ROWS, CY, CZ), 0, NMAT), jax.random.fold_in(arg_keys[5], 1), 0, NMAT - 1).astype(jnp.int32),
        "pml_depth": place_ends(jax.random.randint(arg_keys[6], (ROWS, CY, CZ), 0, 5), jax.random.fold_in(arg_keys[6], 1), 0, 4).astype(jnp.int32),
        "design_start": place_ends(jax.random.randint(arg_keys[7], (N_TILE,), 0, CZ - DZ + 1), jax.random.fold_in(arg_keys[7], 1), 0, CZ - DZ).astype(jnp.int32),
    }


dt_step = 0.5
depth_scale = 4.0


def to_grid(block):
    depth = block.shape[-1]
    rows = N_TILE // TILE_COLS
    lead = block.shape[:-3]
    count = len(lead)
    shaped = block.reshape(lead + (rows, TILE_COLS, CX, CY, depth))
    order = tuple(range(count)) + (count, count + 2, count + 1, count + 3, count + 4)
    return shaped.transpose(order).reshape(lead + (rows * CX, TILE_COLS * CY, depth))


def from_grid(block):
    depth = block.shape[-1]
    rows = N_TILE // TILE_COLS
    lead = block.shape[:-3]
    count = len(lead)
    shaped = block.reshape(lead + (rows, CX, TILE_COLS, CY, depth))
    order = tuple(range(count)) + (count, count + 2, count + 1, count + 3, count + 4)
    return shaped.transpose(order).reshape(lead + (N_TILE * CX, CY, depth))


def ahead(field, axis):
    widths = [(0, 0), (0, 0), (0, 0)]
    widths[axis] = (0, 1)
    padded = jnp.pad(field, widths)
    return lax.slice_in_dim(padded, 1, field.shape[axis] + 1, axis=axis) - field


def behind(field, axis):
    widths = [(0, 0), (0, 0), (0, 0)]
    widths[axis] = (1, 0)
    padded = jnp.pad(field, widths)
    return field - lax.slice_in_dim(padded, 0, field.shape[axis], axis=axis)


def curl(vector, diff):
    return jnp.stack([diff(vector[2], 1) - diff(vector[1], 2),
                      diff(vector[0], 2) - diff(vector[2], 0),
                      diff(vector[1], 0) - diff(vector[0], 1)])


def coefficients(table, kind, depth):
    kinds = jnp.arange(table.shape[0], dtype=jnp.int32)
    onehot = (kind[None] == kinds[:, None, None, None]).astype(jnp.float32)
    eps = jnp.sum(onehot * table[:, None, None, None], axis=0)
    ramp = depth.astype(jnp.float32) / depth_scale
    sigma = ramp * ramp
    s_e = sigma * dt_step / (2.0 * eps)
    s_h = sigma * dt_step / 2.0
    return ((1.0 - s_e) / (1.0 + s_e), dt_step / (eps * (1.0 + s_e)),
            (1.0 - s_h) / (1.0 + s_h), dt_step / (1.0 + s_h))


def advance(e_field, h_field, coeffs):
    ca, cb, da, db = coeffs
    h_field = da * h_field - db * curl(e_field, ahead)
    e_field = ca * e_field + cb * curl(h_field, behind)
    return e_field, h_field


def slice_tile(block, first):
    return lax.dynamic_slice_in_dim(block, first.astype(jnp.int32), DZ, 2)


def reference(e_forward, h_forward, e_adjoint, h_adjoint, eps_table, material, pml_depth, design_start):
    kind = to_grid(material)
    depth = to_grid(pml_depth)
    starts = design_start.astype(jnp.int32)
    outs_ef, outs_hf, outs_ea, outs_ha = [], [], [], []
    gradient = jnp.zeros((N_TILE * CX, CY, DZ), jnp.float32)
    for wave in range(N_WAVE):
        coeffs = coefficients(eps_table[wave], kind, depth)
        ef = to_grid(e_forward[wave])
        hf = to_grid(h_forward[wave])
        ea = to_grid(e_adjoint[wave])
        ha = to_grid(h_adjoint[wave])
        for step in range(STEPS):
            ef, hf = advance(ef, hf, coeffs)
            ea, ha = advance(ea, ha, coeffs)
            corr = from_grid(jnp.sum(ef * ea, axis=0))
            tiles = corr.reshape(N_TILE, CX, CY, corr.shape[-1])
            sliced = jax.vmap(slice_tile)(tiles, starts)
            gradient = gradient + sliced.reshape(N_TILE * CX, CY, DZ)
        outs_ef.append(from_grid(ef))
        outs_hf.append(from_grid(hf))
        outs_ea.append(from_grid(ea))
        outs_ha.append(from_grid(ha))
    return (jnp.stack(outs_ef), jnp.stack(outs_hf), jnp.stack(outs_ea), jnp.stack(outs_ha),
            gradient)
```

```python
import functools

import jax
import jax.numpy as jnp
from jax import lax
from jax.experimental import pallas as pl
from jax.experimental.pallas import tpu as pltpu
from jax.sharding import PartitionSpec as P

STEPS = 4
DZ = 16
TILE_COLS = 8
HALO = STEPS
KINDS = 14

dt_step = 0.5
depth_scale = 4.0

VMEM = pl.BlockSpec(memory_space=pltpu.VMEM)
SMEM = pl.BlockSpec(memory_space=pltpu.SMEM)
ANY = pl.BlockSpec(memory_space=pl.ANY)


def swap_pairs(count, cols, along_x, odd):
    rows = count // cols
    pairs = []
    for row in range(rows):
        for col in range(cols):
            place, size = (row, rows) if along_x else (col, cols)
            other = place + 1 if place % 2 == odd else place - 1
            if 0 <= other < size:
                target = other * cols + col if along_x else row * cols + other
                pairs.append((row * cols + col, target))
    return pairs


def low_half(shape):
    return lax.broadcasted_iota(jnp.int32, shape, len(shape) - 2) < 4


def staggered(block, by):
    row = lax.broadcasted_iota(jnp.int32, block.shape, 0)
    for bit in range(3):
        moved = pltpu.roll(block, (by << bit) % 128, 1)
        block = jnp.where((row >> bit) % 2 == 1, moved, block)
    return block


def pack_kernel(meta, ef, hf, ea, ha, kind, depth, xa1, xb1, xa2, xb2, yb, ya):
    row_even = lax.rem(meta[1], 2) == 0
    col_even = lax.rem(meta[2], 2) == 0
    cells = ef.shape[1]
    at_a = jnp.where(row_even, cells - HALO, 0)
    at_b = jnp.where(row_even, 0, cells - HALO)
    fields = (ef, hf, ea, ha)
    low = low_half((HALO, 8, 128))

    def source(k, rows, ys):
        if k < 12:
            return fields[k // 3][k % 3, rows, ys, :]
        return (kind, depth)[k - 12][rows, ys, :].astype(jnp.float32)

    for k in range(KINDS):
        for at, first, second in ((at_a, xa1, xa2), (at_b, xb1, xb2)):
            rows = pl.ds(at, HALO)
            t0 = source(k, rows, slice(0, 8))
            t1 = source(k, rows, slice(8, 16))
            first[k] = jnp.where(low, t0, t1)
            second[k] = jnp.where(low, t1, t0)

    every = slice(None)

    @pl.when(col_even)
    def _():
        for k in range(KINDS):
            yb[k] = source(k, every, slice(0, 4))
            ya[k] = source(k, every, slice(12, 16))

    @pl.when(jnp.logical_not(col_even))
    def _():
        for k in range(KINDS):
            yb[k] = source(k, every, slice(12, 16))
            ya[k] = source(k, every, slice(0, 4))


def pack(meta, fields, kind, depth):
    cells = kind.shape[0]
    edge = jax.ShapeDtypeStruct((KINDS, HALO, 8, 128), jnp.float32)
    strip = jax.ShapeDtypeStruct((KINDS, cells, 4, 128), jnp.float32)
    return pl.pallas_call(
        pack_kernel,
        out_shape=(edge, edge, edge, edge, strip, strip),
        in_specs=[SMEM] + [VMEM] * 6,
        out_specs=[VMEM] * 6,
        compiler_params=pltpu.CompilerParams(vmem_limit_bytes=16 * 2**20),
        name="pack",
    )(meta, *fields, kind, depth)


def corner_kernel(meta, ra1, rb1, ya, cb, yac):
    col_even = lax.rem(meta[2], 2) == 0
    cells = ya.shape[1]
    yac[:, 0:cells] = ya[...]

    def put(to_a, to_b):
        for k in range(KINDS):
            yac[k, cells:cells + HALO] = ra1[k, :, to_a, :]
            yac[k, cells + HALO:cells + 2 * HALO] = rb1[k, :, to_a, :]
            cb[k, 0:HALO] = ra1[k, :, to_b, :]
            cb[k, HALO:2 * HALO] = rb1[k, :, to_b, :]

    @pl.when(col_even)
    def _():
        put(slice(4, 8), slice(0, 4))

    @pl.when(jnp.logical_not(col_even))
    def _():
        put(slice(0, 4), slice(4, 8))


def corners(meta, ra1, rb1, ya):
    cells = ya.shape[1]
    return pl.pallas_call(
        corner_kernel,
        out_shape=(
            jax.ShapeDtypeStruct((KINDS, 2 * HALO, 4, 128), jnp.float32),
            jax.ShapeDtypeStruct((KINDS, cells + 2 * HALO, 4, 128), jnp.float32),
        ),
        in_specs=[SMEM] + [VMEM] * 3,
        out_specs=[VMEM] * 2,
        compiler_params=pltpu.CompilerParams(vmem_limit_bytes=16 * 2**20),
        name="corners",
    )(meta, ra1, rb1, ya)


def steps_kernel(cols, rows, meta, table, ef, hf, ea, ha, kind, depth,
                 ra1, rb1, ra2, rb2, rb, rcb, rya,
                 ef_out, hf_out, ea_out, ha_out, send,
                 field, ca, cb, da, db, total, in_sems, out_sems):
    start, row, col = meta[0], meta[1], meta[2]
    row_even = lax.rem(row, 2) == 0
    col_even = lax.rem(col, 2) == 0
    cells = kind.shape[0]
    wide = cells + 2 * HALO
    own = slice(HALO, HALO + cells)

    loads = []
    for n, source in enumerate((ef, hf, ea, ha)):
        loads.append(pltpu.make_async_copy(
            source, field.at[pl.ds(3 * n, 3), pl.ds(HALO, cells), pl.ds(0, cells), :],
            in_sems.at[n]))
        loads[-1].start()

    off_a = jnp.where(row_even, HALO + cells, 0)
    off_b = jnp.where(row_even, 0, HALO + cells)
    low = low_half((HALO, 8, 128))
    for k in range(KINDS):
        for off, first, second in ((off_a, ra1, ra2), (off_b, rb1, rb2)):
            here = pl.ds(off, HALO)
            edge, mid = first[k], second[k]
            field[k, here, 0:8, :] = jnp.where(low, edge, mid)
            field[k, here, 8:16, :] = jnp.where(low, mid, edge)

    def columns(side_a, side_b):
        for k in range(KINDS):
            field[k, own, side_a, :] = rya[k, 0:cells]
            field[k, pl.ds(off_a, HALO), side_a, :] = rya[k, cells:cells + HALO]
            field[k, pl.ds(off_b, HALO), side_a, :] = rya[k, cells + HALO:wide]
            field[k, own, side_b, :] = rb[k]
            field[k, pl.ds(off_a, HALO), side_b, :] = rcb[k, 0:HALO]
            field[k, pl.ds(off_b, HALO), side_b, :] = rcb[k, HALO:2 * HALO]

    @pl.when(col_even)
    def _():
        columns(slice(16, 20), slice(20, 24))

    @pl.when(jnp.logical_not(col_even))
    def _():
        columns(slice(20, 24), slice(16, 20))

    field[12, own, 0:cells, :] = kind[...].astype(jnp.float32)
    field[13, own, 0:cells, :] = depth[...].astype(jnp.float32)

    eps = [table[0, m] for m in range(4)]
    place = lax.broadcasted_iota(jnp.int32, (wide, 128), 0)
    after = jnp.logical_and(place >= 16, place < 20)
    before = place >= 20
    outside_y = jnp.logical_or(jnp.logical_and(after, col == cols - 1),
                               jnp.logical_and(before, col == 0))

    def coefficient(x, _):
        m = field[12, x]
        ramp = field[13, x] / depth_scale
        e = jnp.where(m < 0.5, eps[0],
                      jnp.where(m < 1.5, eps[1], jnp.where(m < 2.5, eps[2], eps[3])))
        sigma = ramp * ramp
        s_e = sigma * dt_step / (2.0 * e)
        s_h = sigma * dt_step / 2.0
        outside_x = jnp.logical_or(jnp.logical_and(x < HALO, row == 0),
                                   jnp.logical_and(x >= HALO + cells, row == rows - 1))
        outside = jnp.logical_or(outside_y, outside_x)
        ca[x] = (1.0 - s_e) / (1.0 + s_e)
        cb[x] = jnp.where(outside, 0.0, dt_step / (e * (1.0 + s_e)))
        da[x] = (1.0 - s_h) / (1.0 + s_h)
        db[x] = jnp.where(outside, 0.0, dt_step / (1.0 + s_h))
        return 0

    lax.fori_loop(0, wide, coefficient, 0)

    for load in loads:
        load.wait()

    lane = lax.broadcasted_iota(jnp.int32, (wide, 128), 1)
    last_z, first_z = lane == 127, lane == 0

    def up_z(v):
        return jnp.where(last_z, 0.0, pltpu.roll(v, 127, 1))

    def down_z(v):
        return jnp.where(first_z, 0.0, pltpu.roll(v, 1, 1))

    def up_y(v):
        return pltpu.roll(v, wide - 1, 0)

    def down_y(v):
        return pltpu.roll(v, 1, 0)

    def h_row(x, _):
        dax, dbx = da[x], db[x]
        for e, h in ((0, 3), (6, 9)):
            ex, ey, ez = field[e, x], field[e + 1, x], field[e + 2, x]
            ey1, ez1 = field[e + 1, x + 1], field[e + 2, x + 1]
            field[h, x] = dax * field[h, x] - dbx * ((up_y(ez) - ez) - (up_z(ey) - ey))
            field[h + 1, x] = dax * field[h + 1, x] - dbx * ((up_z(ex) - ex) - (ez1 - ez))
            field[h + 2, x] = dax * field[h + 2, x] - dbx * ((ey1 - ey) - (up_y(ex) - ex))
        return 0

    def e_row(x, keep):
        cax, cbx = ca[x], cb[x]
        new = []
        for e, h in ((0, 3), (6, 9)):
            hx, hy, hz = field[h, x], field[h + 1, x], field[h + 2, x]
            hy1, hz1 = field[h + 1, x - 1], field[h + 2, x - 1]
            new.append((
                cax * field[e, x] + cbx * ((hz - down_y(hz)) - (hy - down_z(hy))),
                cax * field[e + 1, x] + cbx * ((hx - down_z(hx)) - (hz - hz1)),
                cax * field[e + 2, x] + cbx * ((hy - hy1) - (hx - down_y(hx))),
            ))
            for n in range(3):
                field[e + n, x] = new[-1][n]
        if keep is not None:
            term = sum(new[0][n][0:16] * new[1][n][0:16] for n in range(3))
            if keep == 0:
                total[x - HALO] = term
            else:
                total[x - HALO] = total[x - HALO] + term
        return 0

    stores = []
    for step in range(STEPS):
        lax.fori_loop(step, wide - 1 - step, h_row, 0)
        if step == STEPS - 1:
            stores += [(3, hf_out), (9, ha_out)]
            for n, (k, out) in enumerate(stores):
                pltpu.make_async_copy(
                    field.at[pl.ds(k, 3), pl.ds(HALO, cells), pl.ds(0, cells), :], out,
                    out_sems.at[n]).start()
        if step < STEPS - 1:
            lax.fori_loop(step + 1, HALO, lambda x, c: e_row(x, None), 0)
            lax.fori_loop(HALO + cells, wide - 1 - step, lambda x, c: e_row(x, None), 0)
        lax.fori_loop(HALO, HALO + cells, lambda x, c: e_row(x, step), 0)

    stores += [(0, ef_out), (6, ea_out)]
    for n, (k, out) in enumerate(stores):
        if n >= 2:
            pltpu.make_async_copy(
                field.at[pl.ds(k, 3), pl.ds(HALO, cells), pl.ds(0, cells), :], out,
                out_sems.at[n]).start()

    sub = lax.broadcasted_iota(jnp.int32, (8, 128), 0)
    mine = lax.broadcasted_iota(jnp.int32, (8, 128), 1) // DZ == sub
    for tile in range(cells * 2 // 8):
        block = jnp.zeros((8, 128), jnp.float32)
        for n in range(8):
            x, half = (tile * 8 + n) // 2, (tile * 8 + n) % 2
            moved = pltpu.roll(total[x, 8 * half:8 * half + 8, :], 128 - start, 1)
            moved = staggered(moved, DZ)
            line = jnp.sum(jnp.where(mine, moved, 0.0), axis=0, keepdims=True)
            block = jnp.where(sub == n, line, block)
        for peer in range(send.shape[0]):
            send[peer, tile * 8:tile * 8 + 8, :] = block

    for n, (k, out) in enumerate(stores):
        pltpu.make_async_copy(
            field.at[pl.ds(k, 3), pl.ds(HALO, cells), pl.ds(0, cells), :], out,
            out_sems.at[n]).wait()


def all_steps(cols, rows, waves, meta, table, fields, kind, depth, halos):
    cells = kind.shape[0]
    wide = cells + 2 * HALO
    out = jax.ShapeDtypeStruct(fields[0].shape, jnp.float32)
    plane = pltpu.VMEM((wide, wide, 128), jnp.float32)
    return pl.pallas_call(
        functools.partial(steps_kernel, cols, rows),
        out_shape=(out, out, out, out,
                   jax.ShapeDtypeStruct((waves, cells * 2, 128), jnp.float32)),
        in_specs=[SMEM, SMEM] + [ANY] * 4 + [VMEM] * 9,
        out_specs=[ANY] * 4 + [VMEM],
        scratch_shapes=[
            pltpu.VMEM((KINDS, wide, wide, 128), jnp.float32),
            plane, plane, plane, plane,
            pltpu.VMEM((cells, cells, 128), jnp.float32),
            pltpu.SemaphoreType.DMA((4,)),
            pltpu.SemaphoreType.DMA((4,)),
        ],
        compiler_params=pltpu.CompilerParams(vmem_limit_bytes=24 * 2**20),
        name="steps",
    )(meta, table, *fields, kind, depth, *halos)


def gradient_kernel(parts, out):
    waves, lines, _ = parts.shape
    whole = parts[0]
    for wave in range(1, waves):
        whole = whole + parts[wave]
    for n in range(lines):
        spread = jnp.broadcast_to(whole[n:n + 1, :], (8, 128))
        moved = staggered(spread, 128 - DZ)
        out[n // 2, 8 * (n % 2):8 * (n % 2) + 8, :] = moved[:, 0:DZ]


def gradient_of(parts):
    cells = parts.shape[1] // 2
    return pl.pallas_call(
        gradient_kernel,
        out_shape=jax.ShapeDtypeStruct((cells, cells, DZ), jnp.float32),
        in_specs=[VMEM],
        out_specs=VMEM,
        compiler_params=pltpu.CompilerParams(vmem_limit_bytes=8 * 2**20),
        name="gradient",
    )(parts)


def per_device(
    e_forward, h_forward, e_adjoint, h_adjoint, eps_table, material, pml_depth, design_start
):
    cols = TILE_COLS
    count = lax.axis_size("tile")
    rows = count // cols
    me = lax.axis_index("tile")
    meta = jnp.stack([design_start[0], me // cols, me % cols]).astype(jnp.int32)
    fields = (e_forward[0], h_forward[0], e_adjoint[0], h_adjoint[0])

    def swap(value, along_x, odd):
        return lax.ppermute(value, "tile", swap_pairs(count, cols, along_x, odd))

    xa1, xb1, xa2, xb2, yb, ya = pack(meta, fields, material, pml_depth)
    ra1 = swap(xa1, True, 0)
    rb1 = swap(xb1, True, 1)
    rb = swap(yb, False, 1)
    ra2 = swap(xa2, True, 0)
    rb2 = swap(xb2, True, 1)
    cb, yac = corners(meta, ra1, rb1, ya)
    rcb = swap(cb, False, 1)
    rya = swap(yac, False, 0)
    *outs, send = all_steps(cols, rows, lax.axis_size("wave"), meta, eps_table, fields,
                            material, pml_depth, (ra1, rb1, ra2, rb2, rb, rcb, rya))
    parts = lax.all_to_all(send, "wave", 0, 0)
    gradient = gradient_of(parts)
    return tuple(out[None] for out in outs) + (gradient,)


def solution(mesh):
    return jax.shard_map(
        per_device,
        mesh=mesh,
        in_specs=(
            P("wave", None, "tile", None, None),
            P("wave", None, "tile", None, None),
            P("wave", None, "tile", None, None),
            P("wave", None, "tile", None, None),
            P("wave", None),
            P("tile", None, None),
            P("tile", None, None),
            P("tile"),
        ),
        out_specs=(
            P("wave", None, "tile", None, None),
            P("wave", None, "tile", None, None),
            P("wave", None, "tile", None, None),
            P("wave", None, "tile", None, None),
            P("tile", None, None),
        ),
        check_vma=False,
    )
```

```python
import functools

import jax
import jax.numpy as jnp
from jax import lax
from jax.experimental import pallas as pl
from jax.experimental.pallas import tpu as pltpu
from jax.sharding import PartitionSpec as P

STEPS = 4
DZ = 16
TILE_COLS = 8
HALO = STEPS
KINDS = 14
CORNER_FLOPS = 2**36

dt_step = 0.5
depth_scale = 4.0

VMEM = pl.BlockSpec(memory_space=pltpu.VMEM)
SMEM = pl.BlockSpec(memory_space=pltpu.SMEM)
HBM = pl.BlockSpec(memory_space=pltpu.HBM)


def swap_pairs(count, cols, along_x, odd):
    rows = count // cols
    pairs = []
    for row in range(rows):
        for col in range(cols):
            place, size = (row, rows) if along_x else (col, cols)
            other = place + 1 if place % 2 == odd else place - 1
            if 0 <= other < size:
                target = other * cols + col if along_x else row * cols + other
                pairs.append((row * cols + col, target))
    return pairs


def low_half(shape):
    return lax.broadcasted_iota(jnp.int32, shape, len(shape) - 2) < 4


def staggered(block, by):
    row = lax.broadcasted_iota(jnp.int32, block.shape, 0)
    for bit in range(3):
        moved = pltpu.roll(block, (by << bit) % 128, 1)
        block = jnp.where((row >> bit) % 2 == 1, moved, block)
    return block


def pack_kernel(meta, ef, hf, ea, ha, kind, depth,
                own, xa1, xb1, xa2, xb2, yb, ya, whole, sems):
    row_even = lax.rem(meta[1], 2) == 0
    col_even = lax.rem(meta[2], 2) == 0
    cells = kind.shape[0]
    at_a = jnp.where(row_even, cells - HALO, 0)
    at_b = jnp.where(row_even, 0, cells - HALO)
    low = low_half((HALO, 8, 128))

    loads = []
    for k in range(12):
        loads.append(pltpu.make_async_copy(
            (ef, hf, ea, ha)[k // 3].at[k % 3], own.at[k], sems.at[k]))
    loads.append(pltpu.make_async_copy(kind, whole.at[0], sems.at[12]))
    loads.append(pltpu.make_async_copy(depth, whole.at[1], sems.at[13]))
    for load in loads:
        load.start()

    for k in range(KINDS):
        loads[k].wait()
        if k >= 12:
            own[k] = whole[k - 12].astype(jnp.float32)
        for at, first, second in ((at_a, xa1, xa2), (at_b, xb1, xb2)):
            rows = pl.ds(at, HALO)
            t0 = own[k, rows, 0:8, :]
            t1 = own[k, rows, 8:16, :]
            first[k] = jnp.where(low, t0, t1)
            second[k] = jnp.where(low, t1, t0)

    def strips(to_a, to_b):
        for k in range(KINDS):
            ya[k] = own[k, :, to_a, :]
            yb[k] = own[k, :, to_b, :]

    @pl.when(col_even)
    def _():
        strips(slice(12, 16), slice(0, 4))

    @pl.when(jnp.logical_not(col_even))
    def _():
        strips(slice(0, 4), slice(12, 16))


def pack(meta, fields, kind, depth):
    cells = kind.shape[0]
    edge = jax.ShapeDtypeStruct((KINDS, HALO, 8, 128), jnp.float32)
    strip = jax.ShapeDtypeStruct((KINDS, cells, 4, 128), jnp.float32)
    return pl.pallas_call(
        pack_kernel,
        out_shape=(jax.ShapeDtypeStruct((KINDS, cells, cells, 128), jnp.float32),
                   edge, edge, edge, edge, strip, strip),
        in_specs=[SMEM] + [HBM] * 6,
        out_specs=[VMEM] * 7,
        scratch_shapes=[
            pltpu.VMEM((2, cells, cells, 128), jnp.int32),
            pltpu.SemaphoreType.DMA((KINDS,)),
        ],
        compiler_params=pltpu.CompilerParams(vmem_limit_bytes=16 * 2**20),
        name="pack",
    )(meta, *(pltpu.with_memory_space_constraint(value, pltpu.HBM)
             for value in (*fields, kind, depth)))


def corner_kernel(meta, ra1, rb1, ya, cb, yac):
    col_even = lax.rem(meta[2], 2) == 0
    cells = ya.shape[1]
    yac[:, 0:cells] = ya[...]

    def put(to_a, to_b):
        for k in range(KINDS):
            yac[k, cells:cells + HALO] = ra1[k, :, to_a, :]
            yac[k, cells + HALO:cells + 2 * HALO] = rb1[k, :, to_a, :]
            cb[k, 0:HALO] = ra1[k, :, to_b, :]
            cb[k, HALO:2 * HALO] = rb1[k, :, to_b, :]

    @pl.when(col_even)
    def _():
        put(slice(4, 8), slice(0, 4))

    @pl.when(jnp.logical_not(col_even))
    def _():
        put(slice(0, 4), slice(4, 8))


def corners(meta, ra1, rb1, ya):
    cells = ya.shape[1]
    return pl.pallas_call(
        corner_kernel,
        out_shape=(
            jax.ShapeDtypeStruct((KINDS, 2 * HALO, 4, 128), jnp.float32),
            jax.ShapeDtypeStruct((KINDS, cells + 2 * HALO, 4, 128), jnp.float32),
        ),
        in_specs=[SMEM] + [VMEM] * 3,
        out_specs=[VMEM] * 2,
        compiler_params=pltpu.CompilerParams(vmem_limit_bytes=16 * 2**20),
        cost_estimate=pl.CostEstimate(flops=CORNER_FLOPS, bytes_accessed=2**20, transcendentals=0),
        name="corners",
    )(meta, ra1, rb1, ya)


def coefficients(m, d, table, outside):
    eps = jnp.where(m < 0.5, table[0, 0],
                    jnp.where(m < 1.5, table[0, 1],
                              jnp.where(m < 2.5, table[0, 2], table[0, 3])))
    ramp = d / depth_scale
    sigma = ramp * ramp
    s_e = sigma * dt_step / (2.0 * eps)
    s_h = sigma * dt_step / 2.0
    return ((1.0 - s_e) / (1.0 + s_e), jnp.where(outside, 0.0, dt_step / (eps * (1.0 + s_e))),
            (1.0 - s_h) / (1.0 + s_h), jnp.where(outside, 0.0, dt_step / (1.0 + s_h)))


def outside_rows(x, cells, row, rows):
    return jnp.logical_or(jnp.logical_and(x < HALO, row == 0),
                          jnp.logical_and(x >= HALO + cells, row == rows - 1))


def halo_rows(row, cells):
    even = lax.rem(row, 2) == 0
    return jnp.where(even, HALO + cells, 0), jnp.where(even, 0, HALO + cells)


def prepare_kernel(rows, meta, table, own, ra1, rb1, ra2, rb2, field, ca, cb, da, db, matter):
    row = meta[1]
    cells = own.shape[1]
    wide = cells + 2 * HALO
    off_a, off_b = halo_rows(row, cells)
    low = low_half((HALO, 8, 128))
    for k in range(KINDS):
        to = field.at[k] if k < 12 else matter.at[k - 12]
        to[HALO:HALO + cells, 0:cells, :] = own[k]
        for off, first, second in ((off_a, ra1, ra2), (off_b, rb1, rb2)):
            here = pl.ds(off, HALO)
            edge, mid = first[k], second[k]
            to[here, 0:8, :] = jnp.where(low, edge, mid)
            to[here, 8:16, :] = jnp.where(low, mid, edge)

    def fill(x, _):
        outside = outside_rows(x, cells, row, rows)
        values = coefficients(matter[0, x], matter[1, x], table, outside)
        for plane, value in zip((ca, cb, da, db), values):
            plane[x, 0:cells, :] = value
        return 0

    lax.fori_loop(0, wide, fill, 0, unroll=2)


def prepare(rows, meta, table, own, halos):
    cells = own.shape[1]
    wide = cells + 2 * HALO
    plane = jax.ShapeDtypeStruct((wide, wide, 128), jnp.float32)
    return pl.pallas_call(
        functools.partial(prepare_kernel, rows),
        out_shape=(jax.ShapeDtypeStruct((12, wide, wide, 128), jnp.float32),
                   plane, plane, plane, plane),
        in_specs=[SMEM, SMEM] + [VMEM] * 5,
        out_specs=[VMEM] * 5,
        scratch_shapes=[pltpu.VMEM((2, wide, cells, 128), jnp.float32)],
        compiler_params=pltpu.CompilerParams(vmem_limit_bytes=16 * 2**20),
        cost_estimate=pl.CostEstimate(flops=2**36, bytes_accessed=2**22, transcendentals=0),
        name="prepare",
    )(meta, table, own, *halos)


def steps_kernel(cols, rows, meta, table, field_in, ca_in, cb_in, da_in, db_in, rb, rcb, rya,
                 ef_out, hf_out, ea_out, ha_out, send, field, ca, cb, da, db, total, matter):
    start, row, col = meta[0], meta[1], meta[2]
    col_even = lax.rem(col, 2) == 0
    cells = rb.shape[1]
    wide = cells + 2 * HALO
    own = slice(HALO, HALO + cells)
    off_a, off_b = halo_rows(row, cells)

    def columns(first_a, first_b):
        for k in range(KINDS):
            to, base = (field.at[k], cells) if k < 12 else (matter.at[k - 12], 0)
            side_a = slice(base + first_a, base + first_a + 4)
            side_b = slice(base + first_b, base + first_b + 4)
            to[own, side_a, :] = rya[k, 0:cells]
            to[pl.ds(off_a, HALO), side_a, :] = rya[k, cells:cells + HALO]
            to[pl.ds(off_b, HALO), side_a, :] = rya[k, cells + HALO:wide]
            to[own, side_b, :] = rb[k]
            to[pl.ds(off_a, HALO), side_b, :] = rcb[k, 0:HALO]
            to[pl.ds(off_b, HALO), side_b, :] = rcb[k, HALO:2 * HALO]

    @pl.when(col_even)
    def _():
        columns(0, 4)

    @pl.when(jnp.logical_not(col_even))
    def _():
        columns(4, 0)

    after = low_half((8, 128))
    outside_y = jnp.logical_or(jnp.logical_and(after, col == cols - 1),
                               jnp.logical_and(jnp.logical_not(after), col == 0))

    def fill(x, _):
        outside = jnp.logical_or(outside_y, outside_rows(x, cells, row, rows))
        values = coefficients(matter[0, x], matter[1, x], table, outside)
        for plane, value in zip((ca, cb, da, db), values):
            plane[x, cells:wide, :] = value
        return 0

    lax.fori_loop(0, wide, fill, 0, unroll=4)

    lane = lax.broadcasted_iota(jnp.int32, (wide, 128), 1)
    last_z, first_z = lane == 127, lane == 0

    def up_z(v):
        return jnp.where(last_z, 0.0, pltpu.roll(v, 127, 1))

    def down_z(v):
        return jnp.where(first_z, 0.0, pltpu.roll(v, 1, 1))

    def up_y(v):
        return pltpu.roll(v, wide - 1, 0)

    def down_y(v):
        return pltpu.roll(v, 1, 0)

    def h_new(e, h, x, dax, dbx):
        ex, ey, ez = field[e, x], field[e + 1, x], field[e + 2, x]
        ey1, ez1 = field[e + 1, x + 1], field[e + 2, x + 1]
        return (dax * field[h, x] - dbx * ((up_y(ez) - ez) - (up_z(ey) - ey)),
                dax * field[h + 1, x] - dbx * ((up_z(ex) - ex) - (ez1 - ez)),
                dax * field[h + 2, x] - dbx * ((ey1 - ey) - (up_y(ex) - ex)))

    def e_new(e, x, cax, cbx, now, before):
        hx, hy, hz = now
        hy1, hz1 = before
        return (cax * field[e, x] + cbx * ((hz - down_y(hz)) - (hy - down_z(hy))),
                cax * field[e + 1, x] + cbx * ((hx - down_z(hx)) - (hz - hz1)),
                cax * field[e + 2, x] + cbx * ((hy - hy1) - (hx - down_y(hx))))

    outs = {0: ef_out, 3: hf_out, 6: ea_out, 9: ha_out}

    def two_rows(step, i, _):
        x0 = step + 1 + 2 * i
        es = []
        for e, h in ((0, 3), (6, 9)):
            hs, news = [], []
            before = field[h + 1, x0 - 1], field[h + 2, x0 - 1]
            for u in range(2):
                x = x0 + u
                hs.append(h_new(e, h, x, da[x], db[x]))
                news.append(e_new(e, x, ca[x], cb[x], hs[-1], before))
                before = hs[-1][1:]
            for u in range(2):
                for k, new in ((h, hs[u]), (e, news[u])):
                    for n in range(3):
                        if step == STEPS - 1:
                            outs[k][n, x0 + u - HALO] = new[n][0:cells]
                            if k == h and u == 1 and n > 0:
                                field[k + n, x0 + u] = new[n]
                        else:
                            field[k + n, x0 + u] = new[n]
            es.append(news)
        for u in range(2):
            term = sum(es[0][u][n][0:cells] * es[1][u][n][0:cells] for n in range(3))
            total[x0 + u] = term if step == 0 else total[x0 + u] + term
        return 0

    for step in range(STEPS):
        for e, h in ((0, 3), (6, 9)):
            first = h_new(e, h, step, da[step], db[step])
            for n in range(3):
                field[h + n, step] = first[n]
        lax.fori_loop(0, (wide - 2 - 2 * step) // 2, functools.partial(two_rows, step), 0,
                      unroll=2)

    sub = lax.broadcasted_iota(jnp.int32, (8, 128), 0)
    mine = lax.broadcasted_iota(jnp.int32, (8, 128), 1) // DZ == sub
    for tile in range(cells * 2 // 8):
        block = jnp.zeros((8, 128), jnp.float32)
        for n in range(8):
            x, half = HALO + (tile * 8 + n) // 2, (tile * 8 + n) % 2
            moved = pltpu.roll(total[x, 8 * half:8 * half + 8, :], 128 - start, 1)
            line = jnp.sum(jnp.where(mine, staggered(moved, DZ), 0.0), axis=0, keepdims=True)
            block = jnp.where(sub == n, line, block)
        for peer in range(send.shape[0]):
            send[peer, tile * 8:tile * 8 + 8, :] = block


def all_steps(cols, rows, waves, meta, table, state, halos):
    wide = state[0].shape[1]
    cells = wide - 2 * HALO
    out = jax.ShapeDtypeStruct((3, cells, cells, 128), jnp.float32)
    plane = jax.ShapeDtypeStruct((wide, wide, 128), jnp.float32)
    return pl.pallas_call(
        functools.partial(steps_kernel, cols, rows),
        out_shape=(out, out, out, out,
                   jax.ShapeDtypeStruct((waves, cells * 2, 128), jnp.float32),
                   jax.ShapeDtypeStruct((12, wide, wide, 128), jnp.float32),
                   plane, plane, plane, plane),
        in_specs=[SMEM, SMEM] + [VMEM] * 8,
        out_specs=[VMEM] * 10,
        scratch_shapes=[
            pltpu.VMEM((wide, cells, 128), jnp.float32),
            pltpu.VMEM((2, wide, 8, 128), jnp.float32),
        ],
        input_output_aliases={2: 5, 3: 6, 4: 7, 5: 8, 6: 9},
        compiler_params=pltpu.CompilerParams(vmem_limit_bytes=16 * 2**20),
        name="steps",
    )(meta, table, *state, *halos)[:5]


def gradient_kernel(parts, out):
    waves, lines, _ = parts.shape
    whole = parts[0]
    for wave in range(1, waves):
        whole = whole + parts[wave]
    for n in range(lines):
        spread = jnp.broadcast_to(whole[n:n + 1, :], (8, 128))
        moved = staggered(spread, 128 - DZ)
        out[n // 2, 8 * (n % 2):8 * (n % 2) + 8, :] = moved[:, 0:DZ]


def gradient_of(parts):
    cells = parts.shape[1] // 2
    return pl.pallas_call(
        gradient_kernel,
        out_shape=jax.ShapeDtypeStruct((cells, cells, DZ), jnp.float32),
        in_specs=[VMEM],
        out_specs=VMEM,
        compiler_params=pltpu.CompilerParams(vmem_limit_bytes=8 * 2**20),
        name="gradient",
    )(parts)


def per_device(
    e_forward, h_forward, e_adjoint, h_adjoint, eps_table, material, pml_depth, design_start
):
    cols = TILE_COLS
    count = lax.axis_size("tile")
    rows = count // cols
    me = lax.axis_index("tile")
    meta = jnp.stack([design_start[0], me // cols, me % cols]).astype(jnp.int32)
    fields = (e_forward[0], h_forward[0], e_adjoint[0], h_adjoint[0])

    def swap(value, along_x, odd):
        return lax.ppermute(value, "tile", swap_pairs(count, cols, along_x, odd))

    own, xa1, xb1, xa2, xb2, yb, ya = pack(meta, fields, material, pml_depth)
    ra1 = swap(xa1, True, 0)
    rb1 = swap(xb1, True, 1)
    rb = swap(yb, False, 1)
    ra2 = swap(xa2, True, 0)
    rb2 = swap(xb2, True, 1)
    cb, yac = corners(meta, ra1, rb1, ya)
    rcb = swap(cb, False, 1)
    rya = swap(yac, False, 0)
    state = prepare(rows, meta, eps_table, own, (ra1, rb1, ra2, rb2))
    *outs, send = all_steps(cols, rows, lax.axis_size("wave"), meta, eps_table, state,
                            (rb, rcb, rya))
    parts = lax.all_to_all(send, "wave", 0, 0)
    gradient = gradient_of(parts)
    return tuple(out[None] for out in outs) + (gradient,)


def solution(mesh):
    return jax.shard_map(
        per_device,
        mesh=mesh,
        in_specs=(
            P("wave", None, "tile", None, None),
            P("wave", None, "tile", None, None),
            P("wave", None, "tile", None, None),
            P("wave", None, "tile", None, None),
            P("wave", None),
            P("tile", None, None),
            P("tile", None, None),
            P("tile"),
        ),
        out_specs=(
            P("wave", None, "tile", None, None),
            P("wave", None, "tile", None, None),
            P("wave", None, "tile", None, None),
            P("wave", None, "tile", None, None),
            P("tile", None, None),
        ),
        check_vma=False,
    )
```

```python
import functools

import jax
import jax.numpy as jnp
from jax import lax
from jax.experimental import pallas as pl
from jax.experimental.pallas import tpu as pltpu
from jax.sharding import PartitionSpec as P

STEPS = 4
DZ = 16
TILE_COLS = 8
HALO = STEPS
KINDS = 14
UNROLL = 5
CORNER_FLOPS = 2**36
LOAD_FLOPS = 2**30
PREPARE_FLOPS = 2**36

dt_step = 0.5
depth_scale = 4.0

VMEM = pl.BlockSpec(memory_space=pltpu.VMEM)
SMEM = pl.BlockSpec(memory_space=pltpu.SMEM)
HBM = pl.BlockSpec(memory_space=pltpu.HBM)
ANY = pl.BlockSpec(memory_space=pl.ANY)


def swap_pairs(count, cols, along_x, odd):
    rows = count // cols
    pairs = []
    for row in range(rows):
        for col in range(cols):
            place, size = (row, rows) if along_x else (col, cols)
            other = place + 1 if place % 2 == odd else place - 1
            if 0 <= other < size:
                target = other * cols + col if along_x else row * cols + other
                pairs.append((row * cols + col, target))
    return pairs


def low_half(shape):
    return lax.broadcasted_iota(jnp.int32, shape, len(shape) - 2) < 4


def staggered(block, by):
    row = lax.broadcasted_iota(jnp.int32, block.shape, 0)
    for bit in range(3):
        moved = pltpu.roll(block, (by << bit) % 128, 1)
        block = jnp.where((row >> bit) % 2 == 1, moved, block)
    return block


DEEP = (0, 1, 2, 4, 5, 6, 7, 8, 10, 11, 13)
SHALLOW = (3, 9, 12)
LAYERS = 4 * len(DEEP) + 3 * len(SHALLOW)


def layer_places():
    places = [(k, 4 * n, 4) for n, k in enumerate(DEEP)]
    return places + [(k, 4 * len(DEEP) + 3 * n, 3) for n, k in enumerate(SHALLOW)]


def tile_place(cols):
    me = lax.axis_index("tile")
    return lax.div(me, cols), lax.rem(me, cols)


def is_even(place):
    return lax.rem(place, 2) == 0


def edges_kernel(cols, ef, hf, ea, ha, kind, depth, xa, xb, whole, sems):
    row, _ = tile_place(cols)
    cells = kind.shape[0]
    sources = [(ef, hf, ea, ha)[k // 3].at[k % 3] for k in range(12)] + [kind, depth]
    loads = []
    for side, to in enumerate((xa, xb)):
        at_end = is_even(row) if side == 0 else jnp.logical_not(is_even(row))
        for k, place, count in layer_places():
            at = jnp.where(at_end, cells - count, 0)
            target = to.at[pl.ds(place, count)]
            if k >= 12:
                target = whole.at[2 * side + k - 12, pl.ds(0, count)]
            loads.append(pltpu.make_async_copy(
                sources[k].at[pl.ds(at, count)], target, sems.at[side * KINDS + k]))
            loads[-1].start()
    for load in loads:
        load.wait()
    for side, to in enumerate((xa, xb)):
        for k, place, count in layer_places():
            if k >= 12:
                to[place:place + count] = whole[2 * side + k - 12, 0:count].astype(jnp.float32)


def in_hbm(values):
    return [pltpu.with_memory_space_constraint(value, pltpu.HBM) for value in values]


def edges(cols, fields, kind, depth):
    cells = kind.shape[0]
    layers = jax.ShapeDtypeStruct((LAYERS, cells, 128), jnp.float32)
    return pl.pallas_call(
        functools.partial(edges_kernel, cols),
        out_shape=(layers, layers),
        in_specs=[HBM] * 6,
        out_specs=[VMEM] * 2,
        scratch_shapes=[
            pltpu.VMEM((4, HALO, cells, 128), jnp.int32),
            pltpu.SemaphoreType.DMA((2 * KINDS,)),
        ],
        compiler_params=pltpu.CompilerParams(vmem_limit_bytes=16 * 2**20),
        cost_estimate=pl.CostEstimate(flops=2**20, bytes_accessed=2**20, transcendentals=0),
        name="edges",
    )(*in_hbm((*fields, kind, depth)))


def load_kernel(cols, eps_table, ef, hf, ea, ha, kind, depth, after,
                field, ca, cb, da, db, ya, yb, spread, whole, few, sems):
    _, col = tile_place(cols)
    cells = kind.shape[0]
    own = pl.ds(HALO, cells)
    loads = []
    for n, k in enumerate((12, 13) + tuple(range(12))):
        source = (kind, depth)[k - 12] if k >= 12 else (ef, hf, ea, ha)[k // 3].at[k % 3]
        target = whole.at[k - 12] if k >= 12 else field.at[k, own, pl.ds(0, cells), :]
        loads.append(pltpu.make_async_copy(source, target, sems.at[k]))
        loads[-1].start()
    loads.append(pltpu.make_async_copy(eps_table, few, sems.at[KINDS]))
    loads[-1].start()
    for n in (0, 1, -1):
        loads[n].wait()
    table = [few[0, m] for m in range(spread.shape[0])]
    for m, eps in enumerate(table):
        spread[m] = jnp.full(spread.shape[1:], eps, jnp.float32)

    def fill(x, _):
        values = coefficients(whole[0, x].astype(jnp.float32), whole[1, x].astype(jnp.float32),
                              table, None)
        for plane, value in zip((ca, cb, da, db), values):
            plane[HALO + x, 0:cells, :] = value
        return 0

    lax.fori_loop(0, cells, fill, 0, unroll=4)
    for load in loads[2:-1]:
        load.wait()

    def strips(to_a, to_b):
        for k in range(KINDS):
            for out, ys in ((ya, to_a), (yb, to_b)):
                strip = (whole[k - 12, :, ys, :].astype(jnp.float32) if k >= 12
                         else field[k, own, ys, :])
                out[k * cells:(k + 1) * cells] = strip

    @pl.when(is_even(col))
    def _():
        strips(slice(12, 16), slice(0, 4))

    @pl.when(jnp.logical_not(is_even(col)))
    def _():
        strips(slice(0, 4), slice(12, 16))


def load(cols, eps_table, fields, kind, depth, after):
    cells = kind.shape[0]
    wide = cells + 2 * HALO
    plane = jax.ShapeDtypeStruct((wide, wide, 128), jnp.float32)
    return pl.pallas_call(
        functools.partial(load_kernel, cols),
        out_shape=(jax.ShapeDtypeStruct((12, wide, wide, 128), jnp.float32),
                   plane, plane, plane, plane,
                   jax.ShapeDtypeStruct((KINDS * cells + 2 * LAYERS, 4, 128), jnp.float32),
                   jax.ShapeDtypeStruct((KINDS * cells, 4, 128), jnp.float32),
                   jax.ShapeDtypeStruct((eps_table.shape[1], 8, 128), jnp.float32)),
        in_specs=[HBM] * 7 + [ANY],
        out_specs=[VMEM] * 8,
        scratch_shapes=[
            pltpu.VMEM((2, cells, cells, 128), jnp.int32),
            pltpu.SMEM(eps_table.shape, jnp.float32),
            pltpu.SemaphoreType.DMA((KINDS + 1,)),
        ],
        compiler_params=pltpu.CompilerParams(vmem_limit_bytes=16 * 2**20),
        cost_estimate=pl.CostEstimate(flops=LOAD_FLOPS, bytes_accessed=2**22, transcendentals=0),
        name="load",
    )(*in_hbm((eps_table, *fields, kind, depth)), after)


def corner_kernel(cols, ra, rb, ya_in, cb, ya):
    _, col = tile_place(cols)
    strips = ya.shape[0] - 2 * LAYERS

    def put(to_a, to_b):
        for n, source in enumerate((ra, rb)):
            cb[n * LAYERS:(n + 1) * LAYERS] = source[:, to_b, :]
            ya[strips + n * LAYERS:strips + (n + 1) * LAYERS] = source[:, to_a, :]

    @pl.when(is_even(col))
    def _():
        put(slice(12, 16), slice(0, 4))

    @pl.when(jnp.logical_not(is_even(col)))
    def _():
        put(slice(0, 4), slice(12, 16))


def corners(cols, ra, rb, ya):
    return pl.pallas_call(
        functools.partial(corner_kernel, cols),
        out_shape=(jax.ShapeDtypeStruct((2 * LAYERS, 4, 128), jnp.float32),
                   jax.ShapeDtypeStruct(ya.shape, jnp.float32)),
        in_specs=[VMEM] * 3,
        out_specs=[VMEM] * 2,
        input_output_aliases={2: 1},
        compiler_params=pltpu.CompilerParams(vmem_limit_bytes=16 * 2**20),
        cost_estimate=pl.CostEstimate(flops=CORNER_FLOPS, bytes_accessed=2**20, transcendentals=0),
        name="corners",
    )(ra, rb, ya)


def coefficients(m, d, table, outside):
    eps = jnp.where(m < 0.5, table[0],
                    jnp.where(m < 1.5, table[1], jnp.where(m < 2.5, table[2], table[3])))
    ramp = d / depth_scale
    sigma = ramp * ramp
    s_e = sigma * dt_step / (2.0 * eps)
    s_h = sigma * dt_step / 2.0
    values = ((1.0 - s_e) / (1.0 + s_e), dt_step / (eps * (1.0 + s_e)),
              (1.0 - s_h) / (1.0 + s_h), dt_step / (1.0 + s_h))
    if outside is None:
        return values
    return (values[0], jnp.where(outside, 0.0, values[1]),
            values[2], jnp.where(outside, 0.0, values[3]))


def spread_table(spread):
    return [spread[m, 0:1, :] for m in range(spread.shape[0])]


def outside_rows(x, cells, row, rows):
    return jnp.logical_or(jnp.logical_and(x < HALO, row == 0),
                          jnp.logical_and(x >= HALO + cells, row == rows - 1))


def halo_places(row, cells):
    even = is_even(row)
    after, before = HALO + cells, 0
    deep = jnp.where(even, after, before), jnp.where(even, before, after)
    shallow = jnp.where(even, after, before + 1), jnp.where(even, before + 1, after)
    return deep, shallow


def prepare_kernel(cols, rows, spread, field_in, ca_in, cb_in, da_in, db_in, ra, rb,
                   field, ca, cb, da, db, matter):
    row, _ = tile_place(cols)
    cells = ra.shape[1]
    table = spread_table(spread)
    deep, shallow = halo_places(row, cells)
    for k, place, count in layer_places():
        for side, layers in enumerate((ra, rb)):
            here = pl.ds((deep if count == HALO else shallow)[side], count)
            to = field.at[k] if k < 12 else matter.at[k - 12]
            to[here, 0:cells, :] = layers[place:place + count]

    def fill(n, _):
        x = jnp.where(n < HALO, n, n + cells)
        values = coefficients(matter[0, x], matter[1, x], table,
                              outside_rows(x, cells, row, rows))
        for plane, value in zip((ca, cb, da, db), values):
            plane[x, 0:cells, :] = value
        return 0

    lax.fori_loop(0, 2 * HALO, fill, 0, unroll=4)


def prepare(cols, rows, spread, state, ra, rb):
    cells = ra.shape[1]
    wide = cells + 2 * HALO
    return pl.pallas_call(
        functools.partial(prepare_kernel, cols, rows),
        out_shape=tuple(jax.ShapeDtypeStruct(part.shape, part.dtype) for part in state),
        in_specs=[VMEM] * 8,
        out_specs=[VMEM] * 5,
        scratch_shapes=[pltpu.VMEM((2, wide, cells, 128), jnp.float32)],
        input_output_aliases={n + 1: n for n in range(5)},
        compiler_params=pltpu.CompilerParams(vmem_limit_bytes=16 * 2**20),
        cost_estimate=pl.CostEstimate(flops=PREPARE_FLOPS, bytes_accessed=2**22, transcendentals=0),
        name="prepare",
    )(spread, *state, ra, rb)


def steps_kernel(cols, rows, first_z, spread, field_in, ca_in, cb_in, da_in, db_in, ryb, rcb, rya,
                 ef_out, hf_out, ea_out, ha_out, send, field, ca, cb, da, db, total, matter):
    start = first_z[0]
    table = spread_table(spread)
    row, col = tile_place(cols)
    wide = ca.shape[0]
    cells = wide - 2 * HALO
    own = slice(HALO, HALO + cells)
    deep, shallow = halo_places(row, cells)

    def columns(first_a, first_b):
        for k in range(KINDS):
            to, base = (field.at[k], cells) if k < 12 else (matter.at[k - 12], 0)
            to[own, base + first_a:base + first_a + 4, :] = rya[k * cells:(k + 1) * cells]
            to[own, base + first_b:base + first_b + 4, :] = ryb[k * cells:(k + 1) * cells]
        for k, place, count in layer_places():
            to, base = (field.at[k], cells) if k < 12 else (matter.at[k - 12], 0)
            for side in range(2):
                here = pl.ds((deep if count == HALO else shallow)[side], count)
                at = side * LAYERS + place
                to[here, base + first_a:base + first_a + 4, :] = (
                    rya[KINDS * cells + at:KINDS * cells + at + count])
                to[here, base + first_b:base + first_b + 4, :] = rcb[at:at + count]

    @pl.when(is_even(col))
    def _():
        columns(0, 4)

    @pl.when(jnp.logical_not(is_even(col)))
    def _():
        columns(4, 0)

    after = low_half((8, 128))
    outside_y = jnp.logical_or(jnp.logical_and(after, col == cols - 1),
                               jnp.logical_and(jnp.logical_not(after), col == 0))

    def fill(x, _):
        outside = jnp.logical_or(outside_y, outside_rows(x, cells, row, rows))
        values = coefficients(matter[0, x], matter[1, x], table, outside)
        for plane, value in zip((ca, cb, da, db), values):
            plane[x, cells:wide, :] = value
        return 0

    lax.fori_loop(0, wide, fill, 0, unroll=4)

    lane = lax.broadcasted_iota(jnp.int32, (wide, 128), 1)
    top_z, bottom_z = lane == 127, lane == 0

    def up_z(v):
        return jnp.where(top_z, 0.0, pltpu.roll(v, 127, 1))

    def down_z(v):
        return jnp.where(bottom_z, 0.0, pltpu.roll(v, 1, 1))

    def up_y(v):
        return pltpu.roll(v, wide - 1, 0)

    def down_y(v):
        return pltpu.roll(v, 1, 0)

    parts = ((0, 3), (6, 9))
    outs = {0: ef_out, 3: hf_out, 6: ea_out, 9: ha_out}

    def h_new(e, h, x):
        dax, dbx = da[x], db[x]
        ex, ey, ez = field[e, x], field[e + 1, x], field[e + 2, x]
        ey1, ez1 = field[e + 1, x + 1], field[e + 2, x + 1]
        return (dax * field[h, x] - dbx * ((up_y(ez) - ez) - (up_z(ey) - ey)),
                dax * field[h + 1, x] - dbx * ((up_z(ex) - ex) - (ez1 - ez)),
                dax * field[h + 2, x] - dbx * ((ey1 - ey) - (up_y(ex) - ex)))

    def e_new(e, h, x):
        cax, cbx = ca[x], cb[x]
        hx, hy, hz = field[h, x], field[h + 1, x], field[h + 2, x]
        hy1, hz1 = field[h + 1, x - 1], field[h + 2, x - 1]
        return (cax * field[e, x] + cbx * ((hz - down_y(hz)) - (hy - down_z(hy))),
                cax * field[e + 1, x] + cbx * ((hx - down_z(hx)) - (hz - hz1)),
                cax * field[e + 2, x] + cbx * ((hy - hy1) - (hx - down_y(hx))))

    def put(k, x, new, last):
        for n in range(3):
            if last:
                outs[k][n, x - HALO] = new[n][0:cells]
            if not last or (k in (3, 9)):
                field[k + n, x] = new[n]

    def h_rows(x0, count, last):
        news = [[h_new(e, h, x0 + u) for u in range(count)] for e, h in parts]
        for (_, h), new in zip(parts, news):
            for u in range(count):
                put(h, x0 + u, new[u], last)

    def e_rows(step, x0, count, ahead):
        last = step == STEPS - 1
        news = []
        for e, h in parts:
            es = [e_new(e, h, x0 + u) for u in range(count)]
            hs = [h_new(e, h, x0 + count + u) for u in range(count)] if ahead else []
            for u in range(count):
                put(e, x0 + u, es[u], last)
            for u in range(len(hs)):
                put(h, x0 + count + u, hs[u], last)
            news.append(es)
        for u in range(count):
            term = sum(news[0][u][n][0:cells] * news[1][u][n][0:cells] for n in range(3))
            total[x0 + u] = term if step == 0 else total[x0 + u] + term

    for step in range(STEPS):
        last = step == STEPS - 1
        pairs = (wide - 2 - 2 * step) // 2
        h_rows(step, 1, False)
        h_rows(step + 1, 2, last)

        def two_rows(i, _):
            e_rows(step, step + 1 + 2 * i, 2, True)
            return 0

        lax.fori_loop(0, pairs - 1, two_rows, 0, unroll=UNROLL)
        e_rows(step, step + 1 + 2 * (pairs - 1), 2, False)

    sub = lax.broadcasted_iota(jnp.int32, (8, 128), 0)
    mine = lax.broadcasted_iota(jnp.int32, (8, 128), 1) // DZ == sub
    for tile in range(cells * 2 // 8):
        block = jnp.zeros((8, 128), jnp.float32)
        for n in range(8):
            x, half = HALO + (tile * 8 + n) // 2, (tile * 8 + n) % 2
            moved = pltpu.roll(total[x, 8 * half:8 * half + 8, :], 128 - start, 1)
            line = jnp.sum(jnp.where(mine, staggered(moved, DZ), 0.0), axis=0, keepdims=True)
            block = jnp.where(sub == n, line, block)
        for peer in range(send.shape[0]):
            send[peer, tile * 8:tile * 8 + 8, :] = block


def all_steps(cols, rows, waves, first_z, spread, state, halos):
    wide = state[0].shape[1]
    cells = wide - 2 * HALO
    out = pltpu.VMEM((3, cells, cells, 128), jnp.float32)
    plane = jax.ShapeDtypeStruct((wide, wide, 128), jnp.float32)
    return pl.pallas_call(
        functools.partial(steps_kernel, cols, rows),
        out_shape=(out, out, out, out,
                   jax.ShapeDtypeStruct((waves, cells * 2, 128), jnp.float32),
                   jax.ShapeDtypeStruct((12, wide, wide, 128), jnp.float32),
                   plane, plane, plane, plane),
        in_specs=[SMEM] + [VMEM] * 9,
        out_specs=[VMEM] * 10,
        scratch_shapes=[
            pltpu.VMEM((wide, cells, 128), jnp.float32),
            pltpu.VMEM((2, wide, 8, 128), jnp.float32),
        ],
        input_output_aliases={2: 5, 3: 6, 4: 7, 5: 8, 6: 9},
        compiler_params=pltpu.CompilerParams(vmem_limit_bytes=16 * 2**20),
        name="steps",
    )(first_z, spread, *state, *halos)[:5]


def gradient_kernel(parts, out):
    waves, lines, _ = parts.shape
    whole = parts[0]
    for wave in range(1, waves):
        whole = whole + parts[wave]
    for n in range(lines):
        spread = jnp.broadcast_to(whole[n:n + 1, :], (8, 128))
        moved = staggered(spread, 128 - DZ)
        out[n // 2, 8 * (n % 2):8 * (n % 2) + 8, :] = moved[:, 0:DZ]


def gradient_of(parts):
    cells = parts.shape[1] // 2
    return pl.pallas_call(
        gradient_kernel,
        out_shape=jax.ShapeDtypeStruct((cells, cells, DZ), jnp.float32),
        in_specs=[VMEM],
        out_specs=VMEM,
        compiler_params=pltpu.CompilerParams(vmem_limit_bytes=8 * 2**20),
        name="gradient",
    )(parts)


def per_device(
    e_forward, h_forward, e_adjoint, h_adjoint, eps_table, material, pml_depth, design_start
):
    cols = TILE_COLS
    count = lax.axis_size("tile")
    rows = count // cols
    fields = (e_forward[0], h_forward[0], e_adjoint[0], h_adjoint[0])

    def swap(value, along_x, odd):
        return lax.ppermute(value, "tile", swap_pairs(count, cols, along_x, odd))

    xa, xb = edges(cols, fields, material, pml_depth)
    ra = swap(xa, True, 0)
    rb = swap(xb, True, 1)
    *state, ya, yb, spread = load(cols, eps_table, fields, material, pml_depth, xa)
    ryb = swap(yb, False, 1)
    cb, ya = corners(cols, ra, rb, ya)
    rcb = swap(cb, False, 1)
    rya = swap(ya, False, 0)
    state = prepare(cols, rows, spread, state, ra, rb)
    *outs, send = all_steps(cols, rows, lax.axis_size("wave"), design_start, spread, state,
                            (ryb, rcb, rya))
    parts = lax.all_to_all(send, "wave", 0, 0)
    gradient = gradient_of(parts)
    return tuple(out[None] for out in outs) + (gradient,)


def solution(mesh):
    return jax.shard_map(
        per_device,
        mesh=mesh,
        in_specs=(
            P("wave", None, "tile", None, None),
            P("wave", None, "tile", None, None),
            P("wave", None, "tile", None, None),
            P("wave", None, "tile", None, None),
            P("wave", None),
            P("tile", None, None),
            P("tile", None, None),
            P("tile"),
        ),
        out_specs=(
            P("wave", None, "tile", None, None),
            P("wave", None, "tile", None, None),
            P("wave", None, "tile", None, None),
            P("wave", None, "tile", None, None),
            P("tile", None, None),
        ),
        check_vma=False,
    )
```

```python
import functools

import jax
import jax.numpy as jnp
from jax import lax
from jax.experimental import pallas as pl
from jax.experimental.pallas import tpu as pltpu
from jax.sharding import PartitionSpec as P

STEPS = 4
DZ = 16
TILE_COLS = 8
HALO = STEPS
KINDS = 14
UNROLL = 5
CORNER_FLOPS = 2**36
LOAD_FLOPS = 2**30
PREPARE_FLOPS = 2**36

dt_step = 0.5
depth_scale = 4.0

VMEM = pl.BlockSpec(memory_space=pltpu.VMEM)
SMEM = pl.BlockSpec(memory_space=pltpu.SMEM)
HBM = pl.BlockSpec(memory_space=pltpu.HBM)
ANY = pl.BlockSpec(memory_space=pl.ANY)


def swap_pairs(count, cols, along_x, odd):
    rows = count // cols
    pairs = []
    for row in range(rows):
        for col in range(cols):
            place, size = (row, rows) if along_x else (col, cols)
            other = place + 1 if place % 2 == odd else place - 1
            if 0 <= other < size:
                target = other * cols + col if along_x else row * cols + other
                pairs.append((row * cols + col, target))
    return pairs


def low_half(shape):
    return lax.broadcasted_iota(jnp.int32, shape, len(shape) - 2) < 4


def staggered(block, by):
    row = lax.broadcasted_iota(jnp.int32, block.shape, 0)
    for bit in range(3):
        moved = pltpu.roll(block, (by << bit) % 128, 1)
        block = jnp.where((row >> bit) % 2 == 1, moved, block)
    return block


DEEP = (0, 1, 2, 4, 5, 6, 7, 8, 10, 11, 13)
SHALLOW = (3, 9, 12)
LAYERS = 4 * len(DEEP) + 3 * len(SHALLOW)


def layer_places():
    places = [(k, 4 * n, 4) for n, k in enumerate(DEEP)]
    return places + [(k, 4 * len(DEEP) + 3 * n, 3) for n, k in enumerate(SHALLOW)]


def tile_place(cols):
    me = lax.axis_index("tile")
    return lax.div(me, cols), lax.rem(me, cols)


def is_even(place):
    return lax.rem(place, 2) == 0


def edges_kernel(cols, ef, hf, ea, ha, kind, depth, xa, xb, whole, sems):
    row, _ = tile_place(cols)
    cells = kind.shape[0]
    sources = [(ef, hf, ea, ha)[k // 3].at[k % 3] for k in range(12)] + [kind, depth]
    loads = []
    for side, to in enumerate((xa, xb)):
        at_end = is_even(row) if side == 0 else jnp.logical_not(is_even(row))
        for k, place, count in layer_places():
            at = jnp.where(at_end, cells - count, 0)
            target = to.at[pl.ds(place, count)]
            if k >= 12:
                target = whole.at[2 * side + k - 12, pl.ds(0, count)]
            loads.append(pltpu.make_async_copy(
                sources[k].at[pl.ds(at, count)], target, sems.at[side * KINDS + k]))
            loads[-1].start()
    for load in loads:
        load.wait()
    for side, to in enumerate((xa, xb)):
        for k, place, count in layer_places():
            if k >= 12:
                to[place:place + count] = whole[2 * side + k - 12, 0:count].astype(jnp.float32)


def in_hbm(values):
    return [pltpu.with_memory_space_constraint(value, pltpu.HBM) for value in values]


def edges(cols, fields, kind, depth):
    cells = kind.shape[0]
    layers = jax.ShapeDtypeStruct((LAYERS, cells, 128), jnp.float32)
    return pl.pallas_call(
        functools.partial(edges_kernel, cols),
        out_shape=(layers, layers),
        in_specs=[HBM] * 6,
        out_specs=[VMEM] * 2,
        scratch_shapes=[
            pltpu.VMEM((4, HALO, cells, 128), jnp.int32),
            pltpu.SemaphoreType.DMA((2 * KINDS,)),
        ],
        compiler_params=pltpu.CompilerParams(vmem_limit_bytes=16 * 2**20),
        cost_estimate=pl.CostEstimate(flops=2**20, bytes_accessed=2**20, transcendentals=0),
        name="edges",
    )(*in_hbm((*fields, kind, depth)))


def load_kernel(cols, eps_table, ef, hf, ea, ha, kind, depth, after,
                field, ca, cb, da, db, ya, yb, spread, whole, few, sems):
    _, col = tile_place(cols)
    cells = kind.shape[0]
    own = pl.ds(HALO, cells)
    loads = []
    for n, k in enumerate((12, 13) + tuple(range(12))):
        source = (kind, depth)[k - 12] if k >= 12 else (ef, hf, ea, ha)[k // 3].at[k % 3]
        target = whole.at[k - 12] if k >= 12 else field.at[k, own, pl.ds(0, cells), :]
        loads.append(pltpu.make_async_copy(source, target, sems.at[k]))
        loads[-1].start()
    loads.append(pltpu.make_async_copy(eps_table, few, sems.at[KINDS]))
    loads[-1].start()
    for n in (0, 1, -1):
        loads[n].wait()
    table = [few[0, m] for m in range(spread.shape[0])]
    for m, eps in enumerate(table):
        spread[m] = jnp.full(spread.shape[1:], eps, jnp.float32)

    def fill(x, _):
        values = coefficients(whole[0, x].astype(jnp.float32), whole[1, x].astype(jnp.float32),
                              table, None)
        for plane, value in zip((ca, cb, da, db), values):
            plane[HALO + x, 0:cells, :] = value
        return 0

    lax.fori_loop(0, cells, fill, 0, unroll=4)
    for load in loads[2:-1]:
        load.wait()

    def strips(to_a, to_b):
        for k in range(KINDS):
            for out, ys in ((ya, to_a), (yb, to_b)):
                strip = (whole[k - 12, :, ys, :].astype(jnp.float32) if k >= 12
                         else field[k, own, ys, :])
                out[k * cells:(k + 1) * cells] = strip

    @pl.when(is_even(col))
    def _():
        strips(slice(12, 16), slice(0, 4))

    @pl.when(jnp.logical_not(is_even(col)))
    def _():
        strips(slice(0, 4), slice(12, 16))


def load(cols, eps_table, fields, kind, depth, after):
    cells = kind.shape[0]
    wide = cells + 2 * HALO
    plane = jax.ShapeDtypeStruct((wide, wide, 128), jnp.float32)
    return pl.pallas_call(
        functools.partial(load_kernel, cols),
        out_shape=(jax.ShapeDtypeStruct((12, wide, wide, 128), jnp.float32),
                   plane, plane, plane, plane,
                   jax.ShapeDtypeStruct((KINDS * cells, 4, 128), jnp.float32),
                   jax.ShapeDtypeStruct((KINDS * cells, 4, 128), jnp.float32),
                   jax.ShapeDtypeStruct((eps_table.shape[1], 8, 128), jnp.float32)),
        in_specs=[HBM] * 7 + [ANY],
        out_specs=[VMEM] * 8,
        scratch_shapes=[
            pltpu.VMEM((2, cells, cells, 128), jnp.int32),
            pltpu.SMEM(eps_table.shape, jnp.float32),
            pltpu.SemaphoreType.DMA((KINDS + 1,)),
        ],
        compiler_params=pltpu.CompilerParams(vmem_limit_bytes=16 * 2**20),
        cost_estimate=pl.CostEstimate(flops=LOAD_FLOPS, bytes_accessed=2**22, transcendentals=0),
        name="load",
    )(*in_hbm((eps_table, *fields, kind, depth)), after)


def corner_kernel(cols, ra, rb, ca, cb):
    _, col = tile_place(cols)

    def put(to_a, to_b):
        for n, source in enumerate((ra, rb)):
            cb[n * LAYERS:(n + 1) * LAYERS] = source[:, to_b, :]
            ca[n * LAYERS:(n + 1) * LAYERS] = source[:, to_a, :]

    @pl.when(is_even(col))
    def _():
        put(slice(12, 16), slice(0, 4))

    @pl.when(jnp.logical_not(is_even(col)))
    def _():
        put(slice(0, 4), slice(12, 16))


def corners(cols, ra, rb):
    corner = jax.ShapeDtypeStruct((2 * LAYERS, HALO, 128), jnp.float32)
    return pl.pallas_call(
        functools.partial(corner_kernel, cols),
        out_shape=(corner, corner),
        in_specs=[VMEM] * 2,
        out_specs=[VMEM] * 2,
        compiler_params=pltpu.CompilerParams(vmem_limit_bytes=16 * 2**20),
        cost_estimate=pl.CostEstimate(flops=CORNER_FLOPS, bytes_accessed=2**20, transcendentals=0),
        name="corners",
    )(ra, rb)


def coefficients(m, d, table, outside):
    eps = jnp.where(m < 0.5, table[0],
                    jnp.where(m < 1.5, table[1], jnp.where(m < 2.5, table[2], table[3])))
    ramp = d / depth_scale
    sigma = ramp * ramp
    s_e = sigma * dt_step / (2.0 * eps)
    s_h = sigma * dt_step / 2.0
    values = ((1.0 - s_e) / (1.0 + s_e), dt_step / (eps * (1.0 + s_e)),
              (1.0 - s_h) / (1.0 + s_h), dt_step / (1.0 + s_h))
    if outside is None:
        return values
    return (values[0], jnp.where(outside, 0.0, values[1]),
            values[2], jnp.where(outside, 0.0, values[3]))


def spread_table(spread):
    return [spread[m, 0:1, :] for m in range(spread.shape[0])]


def outside_rows(x, cells, row, rows):
    return jnp.logical_or(jnp.logical_and(x < HALO, row == 0),
                          jnp.logical_and(x >= HALO + cells, row == rows - 1))


def halo_places(row, cells):
    even = is_even(row)
    after, before = HALO + cells, 0
    deep = jnp.where(even, after, before), jnp.where(even, before, after)
    shallow = jnp.where(even, after, before + 1), jnp.where(even, before + 1, after)
    return deep, shallow


def sides(col, put):
    @pl.when(is_even(col))
    def _():
        put(0, HALO)

    @pl.when(jnp.logical_not(is_even(col)))
    def _():
        put(HALO, 0)


def fill_columns(cols, table, matter, planes, row_of, count, outside):
    _, col = tile_place(cols)
    cells = planes[0].shape[0] - 2 * HALO
    after = low_half((8, 128))
    outside_y = jnp.logical_or(jnp.logical_and(after, col == cols - 1),
                               jnp.logical_and(jnp.logical_not(after), col == 0))

    def fill(n, _):
        x = row_of(n)
        values = coefficients(matter[0, x], matter[1, x], table,
                              jnp.logical_or(outside_y, outside(x)) if outside else outside_y)
        for plane, value in zip(planes, values):
            plane[x, cells:cells + 8, :] = value
        return 0

    lax.fori_loop(0, count, fill, 0, unroll=4)


def rim_row(cells):
    return lambda n: jnp.where(n < HALO, n, n + cells)


def prepare_kernel(cols, rows, spread, field_in, ca_in, cb_in, da_in, db_in, ra, rb, ryb, rya,
                   field, ca, cb, da, db, matter, strip):
    row, col = tile_place(cols)
    cells = ra.shape[1]
    own = slice(HALO, HALO + cells)

    def columns(first_a, first_b):
        for k in range(KINDS):
            to, base = (field.at[k], cells) if k < 12 else (strip.at[k - 12], 0)
            to[own, base + first_a:base + first_a + 4, :] = rya[k * cells:(k + 1) * cells]
            to[own, base + first_b:base + first_b + 4, :] = ryb[k * cells:(k + 1) * cells]

    sides(col, columns)
    fill_columns(cols, spread_table(spread), strip, (ca, cb, da, db), lambda n: n + HALO, cells,
                 None)
    table = spread_table(spread)
    deep, shallow = halo_places(row, cells)
    for k, place, count in layer_places():
        for side, layers in enumerate((ra, rb)):
            here = pl.ds((deep if count == HALO else shallow)[side], count)
            to = field.at[k] if k < 12 else matter.at[k - 12]
            to[here, 0:cells, :] = layers[place:place + count]

    def fill(n, _):
        x = rim_row(cells)(n)
        values = coefficients(matter[0, x], matter[1, x], table,
                              outside_rows(x, cells, row, rows))
        for plane, value in zip((ca, cb, da, db), values):
            plane[x, 0:cells, :] = value
        return 0

    lax.fori_loop(0, 2 * HALO, fill, 0, unroll=4)


def prepare(cols, rows, spread, state, ra, rb, ryb, rya):
    cells = ra.shape[1]
    wide = cells + 2 * HALO
    return pl.pallas_call(
        functools.partial(prepare_kernel, cols, rows),
        out_shape=tuple(jax.ShapeDtypeStruct(part.shape, part.dtype) for part in state),
        in_specs=[VMEM] * 10,
        out_specs=[VMEM] * 5,
        scratch_shapes=[pltpu.VMEM((2, wide, cells, 128), jnp.float32),
                        pltpu.VMEM((2, wide, 8, 128), jnp.float32)],
        input_output_aliases={n + 1: n for n in range(5)},
        compiler_params=pltpu.CompilerParams(vmem_limit_bytes=16 * 2**20),
        cost_estimate=pl.CostEstimate(flops=PREPARE_FLOPS, bytes_accessed=2**22, transcendentals=0),
        name="prepare",
    )(spread, *state, ra, rb, ryb, rya)


def steps_kernel(cols, rows, first_z, spread, field_in, ca_in, cb_in, da_in, db_in, rcb, rca,
                 ef_out, hf_out, ea_out, ha_out, send, field, ca, cb, da, db, total, matter):
    start = first_z[0]
    table = spread_table(spread)
    row, col = tile_place(cols)
    wide = ca.shape[0]
    cells = wide - 2 * HALO
    deep, shallow = halo_places(row, cells)

    def columns(first_a, first_b):
        for k, place, count in layer_places():
            to, base = (field.at[k], cells) if k < 12 else (matter.at[k - 12], 0)
            for side in range(2):
                here = pl.ds((deep if count == HALO else shallow)[side], count)
                at = side * LAYERS + place
                to[here, base + first_a:base + first_a + 4, :] = rca[at:at + count]
                to[here, base + first_b:base + first_b + 4, :] = rcb[at:at + count]

    sides(col, columns)
    fill_columns(cols, table, matter, (ca, cb, da, db), rim_row(cells), 2 * HALO,
                 lambda x: outside_rows(x, cells, row, rows))

    lane = lax.broadcasted_iota(jnp.int32, (wide, 128), 1)
    top_z, bottom_z = lane == 127, lane == 0

    def up_z(v):
        return jnp.where(top_z, 0.0, pltpu.roll(v, 127, 1))

    def down_z(v):
        return jnp.where(bottom_z, 0.0, pltpu.roll(v, 1, 1))

    def up_y(v):
        return pltpu.roll(v, wide - 1, 0)

    def down_y(v):
        return pltpu.roll(v, 1, 0)

    parts = ((0, 3), (6, 9))
    outs = {0: ef_out, 3: hf_out, 6: ea_out, 9: ha_out}

    def h_new(e, h, x):
        dax, dbx = da[x], db[x]
        ex, ey, ez = field[e, x], field[e + 1, x], field[e + 2, x]
        ey1, ez1 = field[e + 1, x + 1], field[e + 2, x + 1]
        return (dax * field[h, x] - dbx * ((up_y(ez) - ez) - (up_z(ey) - ey)),
                dax * field[h + 1, x] - dbx * ((up_z(ex) - ex) - (ez1 - ez)),
                dax * field[h + 2, x] - dbx * ((ey1 - ey) - (up_y(ex) - ex)))

    def e_new(e, h, x):
        cax, cbx = ca[x], cb[x]
        hx, hy, hz = field[h, x], field[h + 1, x], field[h + 2, x]
        hy1, hz1 = field[h + 1, x - 1], field[h + 2, x - 1]
        return (cax * field[e, x] + cbx * ((hz - down_y(hz)) - (hy - down_z(hy))),
                cax * field[e + 1, x] + cbx * ((hx - down_z(hx)) - (hz - hz1)),
                cax * field[e + 2, x] + cbx * ((hy - hy1) - (hx - down_y(hx))))

    def put(k, x, new, last):
        for n in range(3):
            if last:
                outs[k][n, x - HALO] = new[n][0:cells]
            if not last or (k in (3, 9)):
                field[k + n, x] = new[n]

    def h_rows(x0, count, last):
        news = [[h_new(e, h, x0 + u) for u in range(count)] for e, h in parts]
        for (_, h), new in zip(parts, news):
            for u in range(count):
                put(h, x0 + u, new[u], last)

    def e_rows(step, x0, count, ahead):
        last = step == STEPS - 1
        news = []
        for e, h in parts:
            es = [e_new(e, h, x0 + u) for u in range(count)]
            hs = [h_new(e, h, x0 + count + u) for u in range(count)] if ahead else []
            for u in range(count):
                put(e, x0 + u, es[u], last)
            for u in range(len(hs)):
                put(h, x0 + count + u, hs[u], last)
            news.append(es)
        for u in range(count):
            term = sum(news[0][u][n][0:cells] * news[1][u][n][0:cells] for n in range(3))
            total[x0 + u] = term if step == 0 else total[x0 + u] + term

    for step in range(STEPS):
        last = step == STEPS - 1
        pairs = (wide - 2 - 2 * step) // 2
        h_rows(step, 1, False)
        h_rows(step + 1, 2, last)

        def two_rows(i, _):
            e_rows(step, step + 1 + 2 * i, 2, True)
            return 0

        lax.fori_loop(0, pairs - 1, two_rows, 0, unroll=UNROLL)
        e_rows(step, step + 1 + 2 * (pairs - 1), 2, False)

    sub = lax.broadcasted_iota(jnp.int32, (8, 128), 0)
    mine = lax.broadcasted_iota(jnp.int32, (8, 128), 1) // DZ == sub
    for tile in range(cells * 2 // 8):
        block = jnp.zeros((8, 128), jnp.float32)
        for n in range(8):
            x, half = HALO + (tile * 8 + n) // 2, (tile * 8 + n) % 2
            moved = pltpu.roll(total[x, 8 * half:8 * half + 8, :], 128 - start, 1)
            line = jnp.sum(jnp.where(mine, staggered(moved, DZ), 0.0), axis=0, keepdims=True)
            block = jnp.where(sub == n, line, block)
        for peer in range(send.shape[0]):
            send[peer, tile * 8:tile * 8 + 8, :] = block


def all_steps(cols, rows, waves, first_z, spread, state, halos):
    wide = state[0].shape[1]
    cells = wide - 2 * HALO
    out = pltpu.VMEM((3, cells, cells, 128), jnp.float32)
    plane = jax.ShapeDtypeStruct((wide, wide, 128), jnp.float32)
    return pl.pallas_call(
        functools.partial(steps_kernel, cols, rows),
        out_shape=(out, out, out, out,
                   jax.ShapeDtypeStruct((waves, cells * 2, 128), jnp.float32),
                   jax.ShapeDtypeStruct((12, wide, wide, 128), jnp.float32),
                   plane, plane, plane, plane),
        in_specs=[SMEM] + [VMEM] * 8,
        out_specs=[VMEM] * 10,
        scratch_shapes=[
            pltpu.VMEM((wide, cells, 128), jnp.float32),
            pltpu.VMEM((2, wide, 8, 128), jnp.float32),
        ],
        input_output_aliases={2: 5, 3: 6, 4: 7, 5: 8, 6: 9},
        compiler_params=pltpu.CompilerParams(vmem_limit_bytes=16 * 2**20),
        name="steps",
    )(first_z, spread, *state, *halos)[:5]


def gradient_kernel(parts, out):
    waves, lines, _ = parts.shape
    whole = parts[0]
    for wave in range(1, waves):
        whole = whole + parts[wave]
    for n in range(lines):
        spread = jnp.broadcast_to(whole[n:n + 1, :], (8, 128))
        moved = staggered(spread, 128 - DZ)
        out[n // 2, 8 * (n % 2):8 * (n % 2) + 8, :] = moved[:, 0:DZ]


def gradient_of(parts):
    cells = parts.shape[1] // 2
    return pl.pallas_call(
        gradient_kernel,
        out_shape=jax.ShapeDtypeStruct((cells, cells, DZ), jnp.float32),
        in_specs=[VMEM],
        out_specs=VMEM,
        compiler_params=pltpu.CompilerParams(vmem_limit_bytes=8 * 2**20),
        name="gradient",
    )(parts)


def per_device(
    e_forward, h_forward, e_adjoint, h_adjoint, eps_table, material, pml_depth, design_start
):
    cols = TILE_COLS
    count = lax.axis_size("tile")
    rows = count // cols
    fields = (e_forward[0], h_forward[0], e_adjoint[0], h_adjoint[0])

    def swap(value, along_x, odd):
        return lax.ppermute(value, "tile", swap_pairs(count, cols, along_x, odd))

    xa, xb = edges(cols, fields, material, pml_depth)
    ra = swap(xa, True, 0)
    rb = swap(xb, True, 1)
    *state, ya, yb, spread = load(cols, eps_table, fields, material, pml_depth, xa)
    ryb = swap(yb, False, 1)
    rya = swap(ya, False, 0)
    ca, cb = corners(cols, ra, rb)
    rcb = swap(cb, False, 1)
    rca = swap(ca, False, 0)
    state = prepare(cols, rows, spread, state, ra, rb, ryb, rya)
    *outs, send = all_steps(cols, rows, lax.axis_size("wave"), design_start, spread, state,
                            (rcb, rca))
    parts = lax.all_to_all(send, "wave", 0, 0)
    gradient = gradient_of(parts)
    return tuple(out[None] for out in outs) + (gradient,)


def solution(mesh):
    return jax.shard_map(
        per_device,
        mesh=mesh,
        in_specs=(
            P("wave", None, "tile", None, None),
            P("wave", None, "tile", None, None),
            P("wave", None, "tile", None, None),
            P("wave", None, "tile", None, None),
            P("wave", None),
            P("tile", None, None),
            P("tile", None, None),
            P("tile"),
        ),
        out_specs=(
            P("wave", None, "tile", None, None),
            P("wave", None, "tile", None, None),
            P("wave", None, "tile", None, None),
            P("wave", None, "tile", None, None),
            P("tile", None, None),
        ),
        check_vma=False,
    )
```

```python
import functools

import jax
import jax.numpy as jnp
from jax import lax
from jax.experimental import pallas as pl
from jax.experimental.pallas import tpu as pltpu
from jax.sharding import PartitionSpec as P

STEPS = 4
DZ = 16
TILE_COLS = 8
HALO = STEPS
KINDS = 14
UNROLL = 5
CORNER_FLOPS = 2**36
LOAD_FLOPS = 2**30
PREPARE_FLOPS = 2**36

dt_step = 0.5
depth_scale = 4.0

VMEM = pl.BlockSpec(memory_space=pltpu.VMEM)
SMEM = pl.BlockSpec(memory_space=pltpu.SMEM)
HBM = pl.BlockSpec(memory_space=pltpu.HBM)
ANY = pl.BlockSpec(memory_space=pl.ANY)


def swap_pairs(count, cols, along_x, odd):
    rows = count // cols
    pairs = []
    for row in range(rows):
        for col in range(cols):
            place, size = (row, rows) if along_x else (col, cols)
            other = place + 1 if place % 2 == odd else place - 1
            if 0 <= other < size:
                target = other * cols + col if along_x else row * cols + other
                pairs.append((row * cols + col, target))
    return pairs


def low_half(shape):
    return lax.broadcasted_iota(jnp.int32, shape, len(shape) - 2) < 4


DEEP = (0, 1, 2, 4, 5, 6, 7, 8, 10, 11, 13)
SHALLOW = (3, 9, 12)
LAYERS = 4 * len(DEEP) + 3 * len(SHALLOW)


def layer_places():
    places = [(k, 4 * n, 4) for n, k in enumerate(DEEP)]
    return places + [(k, 4 * len(DEEP) + 3 * n, 3) for n, k in enumerate(SHALLOW)]


def tile_place(cols):
    me = lax.axis_index("tile")
    return lax.div(me, cols), lax.rem(me, cols)


def is_even(place):
    return lax.rem(place, 2) == 0


def edges_kernel(cols, ef, hf, ea, ha, kind, depth, xa, xb, whole, sems):
    row, _ = tile_place(cols)
    cells = kind.shape[0]
    sources = [(ef, hf, ea, ha)[k // 3].at[k % 3] for k in range(12)] + [kind, depth]
    loads = []
    for side, to in enumerate((xa, xb)):
        at_end = is_even(row) if side == 0 else jnp.logical_not(is_even(row))
        for k, place, count in layer_places():
            at = jnp.where(at_end, cells - count, 0)
            target = to.at[pl.ds(place, count)]
            if k >= 12:
                target = whole.at[2 * side + k - 12, pl.ds(0, count)]
            loads.append(pltpu.make_async_copy(
                sources[k].at[pl.ds(at, count)], target, sems.at[side * KINDS + k]))
            loads[-1].start()
    for load in loads:
        load.wait()
    for side, to in enumerate((xa, xb)):
        for k, place, count in layer_places():
            if k >= 12:
                to[place:place + count] = whole[2 * side + k - 12, 0:count].astype(jnp.float32)


def in_hbm(values):
    return [pltpu.with_memory_space_constraint(value, pltpu.HBM) for value in values]


def edges(cols, fields, kind, depth):
    cells = kind.shape[0]
    layers = jax.ShapeDtypeStruct((LAYERS, cells, 128), jnp.float32)
    return pl.pallas_call(
        functools.partial(edges_kernel, cols),
        out_shape=(layers, layers),
        in_specs=[HBM] * 6,
        out_specs=[VMEM] * 2,
        scratch_shapes=[
            pltpu.VMEM((4, HALO, cells, 128), jnp.int32),
            pltpu.SemaphoreType.DMA((2 * KINDS,)),
        ],
        compiler_params=pltpu.CompilerParams(vmem_limit_bytes=16 * 2**20),
        cost_estimate=pl.CostEstimate(flops=2**20, bytes_accessed=2**20, transcendentals=0),
        name="edges",
    )(*in_hbm((*fields, kind, depth)))


def load_kernel(cols, eps_table, ef, hf, ea, ha, kind, depth, after,
                field, ca, cb, da, db, ya, yb, spread, whole, few, sems):
    _, col = tile_place(cols)
    cells = kind.shape[0]
    own = pl.ds(HALO, cells)
    loads = []
    for n, k in enumerate((12, 13) + tuple(range(12))):
        source = (kind, depth)[k - 12] if k >= 12 else (ef, hf, ea, ha)[k // 3].at[k % 3]
        target = whole.at[k - 12] if k >= 12 else field.at[k, own, pl.ds(0, cells), :]
        loads.append(pltpu.make_async_copy(source, target, sems.at[k]))
        loads[-1].start()
    loads.append(pltpu.make_async_copy(eps_table, few, sems.at[KINDS]))
    loads[-1].start()
    for n in (0, 1, -1):
        loads[n].wait()
    table = [few[0, m] for m in range(spread.shape[0])]
    for m, eps in enumerate(table):
        spread[m] = jnp.full(spread.shape[1:], eps, jnp.float32)

    def fill(x, _):
        values = coefficients(whole[0, x].astype(jnp.float32), whole[1, x].astype(jnp.float32),
                              table, None)
        for plane, value in zip((ca, cb, da, db), values):
            plane[HALO + x, 0:cells, :] = value
        return 0

    lax.fori_loop(0, cells, fill, 0, unroll=4)
    for load in loads[2:-1]:
        load.wait()

    def strips(to_a, to_b):
        for k in range(KINDS):
            for out, ys in ((ya, to_a), (yb, to_b)):
                strip = (whole[k - 12, :, ys, :].astype(jnp.float32) if k >= 12
                         else field[k, own, ys, :])
                out[k * cells:(k + 1) * cells] = strip

    @pl.when(is_even(col))
    def _():
        strips(slice(12, 16), slice(0, 4))

    @pl.when(jnp.logical_not(is_even(col)))
    def _():
        strips(slice(0, 4), slice(12, 16))


def load(cols, eps_table, fields, kind, depth, after):
    cells = kind.shape[0]
    wide = cells + 2 * HALO
    plane = jax.ShapeDtypeStruct((wide, wide, 128), jnp.float32)
    return pl.pallas_call(
        functools.partial(load_kernel, cols),
        out_shape=(jax.ShapeDtypeStruct((12, wide, wide, 128), jnp.float32),
                   plane, plane, plane, plane,
                   jax.ShapeDtypeStruct((KINDS * cells, 4, 128), jnp.float32),
                   jax.ShapeDtypeStruct((KINDS * cells, 4, 128), jnp.float32),
                   jax.ShapeDtypeStruct((eps_table.shape[1], 8, 128), jnp.float32)),
        in_specs=[HBM] * 7 + [ANY],
        out_specs=[VMEM] * 8,
        scratch_shapes=[
            pltpu.VMEM((2, cells, cells, 128), jnp.int32),
            pltpu.SMEM(eps_table.shape, jnp.float32),
            pltpu.SemaphoreType.DMA((KINDS + 1,)),
        ],
        compiler_params=pltpu.CompilerParams(vmem_limit_bytes=16 * 2**20),
        cost_estimate=pl.CostEstimate(flops=LOAD_FLOPS, bytes_accessed=2**22, transcendentals=0),
        name="load",
    )(*in_hbm((eps_table, *fields, kind, depth)), after)


def corner_kernel(cols, ra, rb, ca, cb):
    _, col = tile_place(cols)

    def put(to_a, to_b):
        for n, source in enumerate((ra, rb)):
            cb[n * LAYERS:(n + 1) * LAYERS] = source[:, to_b, :]
            ca[n * LAYERS:(n + 1) * LAYERS] = source[:, to_a, :]

    @pl.when(is_even(col))
    def _():
        put(slice(12, 16), slice(0, 4))

    @pl.when(jnp.logical_not(is_even(col)))
    def _():
        put(slice(0, 4), slice(12, 16))


def corners(cols, ra, rb):
    corner = jax.ShapeDtypeStruct((2 * LAYERS, HALO, 128), jnp.float32)
    return pl.pallas_call(
        functools.partial(corner_kernel, cols),
        out_shape=(corner, corner),
        in_specs=[VMEM] * 2,
        out_specs=[VMEM] * 2,
        compiler_params=pltpu.CompilerParams(vmem_limit_bytes=16 * 2**20),
        cost_estimate=pl.CostEstimate(flops=CORNER_FLOPS, bytes_accessed=2**20, transcendentals=0),
        name="corners",
    )(ra, rb)


def coefficients(m, d, table, outside):
    eps = jnp.where(m < 0.5, table[0],
                    jnp.where(m < 1.5, table[1], jnp.where(m < 2.5, table[2], table[3])))
    ramp = d / depth_scale
    sigma = ramp * ramp
    s_e = sigma * dt_step / (2.0 * eps)
    s_h = sigma * dt_step / 2.0
    values = ((1.0 - s_e) / (1.0 + s_e), dt_step / (eps * (1.0 + s_e)),
              (1.0 - s_h) / (1.0 + s_h), dt_step / (1.0 + s_h))
    if outside is None:
        return values
    return (values[0], jnp.where(outside, 0.0, values[1]),
            values[2], jnp.where(outside, 0.0, values[3]))


def spread_table(spread):
    return [spread[m, 0:1, :] for m in range(spread.shape[0])]


def outside_rows(x, cells, row, rows):
    return jnp.logical_or(jnp.logical_and(x < HALO, row == 0),
                          jnp.logical_and(x >= HALO + cells, row == rows - 1))


def halo_places(row, cells):
    even = is_even(row)
    after, before = HALO + cells, 0
    deep = jnp.where(even, after, before), jnp.where(even, before, after)
    shallow = jnp.where(even, after, before + 1), jnp.where(even, before + 1, after)
    return deep, shallow


def sides(col, put):
    @pl.when(is_even(col))
    def _():
        put(0, HALO)

    @pl.when(jnp.logical_not(is_even(col)))
    def _():
        put(HALO, 0)


def fill_columns(cols, table, matter, planes, row_of, count, outside):
    _, col = tile_place(cols)
    cells = planes[0].shape[0] - 2 * HALO
    after = low_half((8, 128))
    outside_y = jnp.logical_or(jnp.logical_and(after, col == cols - 1),
                               jnp.logical_and(jnp.logical_not(after), col == 0))

    def fill(n, _):
        x = row_of(n)
        values = coefficients(matter[0, x], matter[1, x], table,
                              jnp.logical_or(outside_y, outside(x)) if outside else outside_y)
        for plane, value in zip(planes, values):
            plane[x, cells:cells + 8, :] = value
        return 0

    lax.fori_loop(0, count, fill, 0, unroll=4)


def rim_row(cells):
    return lambda n: jnp.where(n < HALO, n, n + cells)


def prepare_kernel(cols, rows, spread, field_in, ca_in, cb_in, da_in, db_in, ra, rb, ryb, rya,
                   field, ca, cb, da, db, matter, strip):
    row, col = tile_place(cols)
    cells = ra.shape[1]
    own = slice(HALO, HALO + cells)

    def columns(first_a, first_b):
        for k in range(KINDS):
            to, base = (field.at[k], cells) if k < 12 else (strip.at[k - 12], 0)
            to[own, base + first_a:base + first_a + 4, :] = rya[k * cells:(k + 1) * cells]
            to[own, base + first_b:base + first_b + 4, :] = ryb[k * cells:(k + 1) * cells]

    sides(col, columns)
    fill_columns(cols, spread_table(spread), strip, (ca, cb, da, db), lambda n: n + HALO, cells,
                 None)
    table = spread_table(spread)
    deep, shallow = halo_places(row, cells)
    for k, place, count in layer_places():
        for side, layers in enumerate((ra, rb)):
            here = pl.ds((deep if count == HALO else shallow)[side], count)
            to = field.at[k] if k < 12 else matter.at[k - 12]
            to[here, 0:cells, :] = layers[place:place + count]

    def fill(n, _):
        x = rim_row(cells)(n)
        values = coefficients(matter[0, x], matter[1, x], table,
                              outside_rows(x, cells, row, rows))
        for plane, value in zip((ca, cb, da, db), values):
            plane[x, 0:cells, :] = value
        return 0

    lax.fori_loop(0, 2 * HALO, fill, 0, unroll=4)


def prepare(cols, rows, spread, state, ra, rb, ryb, rya):
    cells = ra.shape[1]
    wide = cells + 2 * HALO
    return pl.pallas_call(
        functools.partial(prepare_kernel, cols, rows),
        out_shape=tuple(jax.ShapeDtypeStruct(part.shape, part.dtype) for part in state),
        in_specs=[VMEM] * 10,
        out_specs=[VMEM] * 5,
        scratch_shapes=[pltpu.VMEM((2, wide, cells, 128), jnp.float32),
                        pltpu.VMEM((2, wide, 8, 128), jnp.float32)],
        input_output_aliases={n + 1: n for n in range(5)},
        compiler_params=pltpu.CompilerParams(vmem_limit_bytes=16 * 2**20),
        cost_estimate=pl.CostEstimate(flops=PREPARE_FLOPS, bytes_accessed=2**22, transcendentals=0),
        name="prepare",
    )(spread, *state, ra, rb, ryb, rya)


def steps_kernel(cols, rows, first_z, spread, field_in, ca_in, cb_in, da_in, db_in, rcb, rca,
                 ef_out, hf_out, ea_out, ha_out, send, field, ca, cb, da, db, total, matter):
    start = first_z[0]
    table = spread_table(spread)
    row, col = tile_place(cols)
    wide = ca.shape[0]
    cells = wide - 2 * HALO
    deep, shallow = halo_places(row, cells)

    def columns(first_a, first_b):
        for k, place, count in layer_places():
            to, base = (field.at[k], cells) if k < 12 else (matter.at[k - 12], 0)
            for side in range(2):
                here = pl.ds((deep if count == HALO else shallow)[side], count)
                at = side * LAYERS + place
                to[here, base + first_a:base + first_a + 4, :] = rca[at:at + count]
                to[here, base + first_b:base + first_b + 4, :] = rcb[at:at + count]

    sides(col, columns)
    fill_columns(cols, table, matter, (ca, cb, da, db), rim_row(cells), 2 * HALO,
                 lambda x: outside_rows(x, cells, row, rows))

    lane = lax.broadcasted_iota(jnp.int32, (wide, 128), 1)
    top_z, bottom_z = lane == 127, lane == 0

    def up_z(v):
        return jnp.where(top_z, 0.0, pltpu.roll(v, 127, 1))

    def down_z(v):
        return jnp.where(bottom_z[0:v.shape[0]], 0.0, pltpu.roll(v, 1, 1))

    def up_y(v):
        return pltpu.roll(v, wide - 1, 0)

    def down_y(v):
        return pltpu.roll(v, 1, 0)

    parts = ((0, 3), (6, 9))
    outs = {0: ef_out, 3: hf_out, 6: ea_out, 9: ha_out}

    def h_new(e, h, x):
        dax, dbx = da[x], db[x]
        ex, ey, ez = field[e, x], field[e + 1, x], field[e + 2, x]
        ey1, ez1 = field[e + 1, x + 1], field[e + 2, x + 1]
        return (dax * field[h, x] - dbx * ((up_y(ez) - ez) - (up_z(ey) - ey)),
                dax * field[h + 1, x] - dbx * ((up_z(ex) - ex) - (ez1 - ez)),
                dax * field[h + 2, x] - dbx * ((ey1 - ey) - (up_y(ex) - ex)))

    def e_new(e, h, x, last):
        ys = cells if last else wide
        cax, cbx = ca[x, 0:ys], cb[x, 0:ys]
        all_hx, hy, all_hz = field[h, x], field[h + 1, x, 0:ys], field[h + 2, x]
        hx, hz = all_hx[0:ys], all_hz[0:ys]
        hy1, hz1 = field[h + 1, x - 1, 0:ys], field[h + 2, x - 1, 0:ys]
        return (cax * field[e, x, 0:ys] + cbx * ((hz - down_y(all_hz)[0:ys]) - (hy - down_z(hy))),
                cax * field[e + 1, x, 0:ys] + cbx * ((hx - down_z(hx)) - (hz - hz1)),
                cax * field[e + 2, x, 0:ys] + cbx * ((hy - hy1) - (hx - down_y(all_hx)[0:ys])))

    def put(k, x, new, last):
        for n in range(3):
            if last:
                outs[k][n, x - HALO] = new[n][0:cells]
            if not last or (k in (3, 9)):
                field[k + n, x] = new[n]

    def h_rows(x0, count, last):
        news = [[h_new(e, h, x0 + u) for u in range(count)] for e, h in parts]
        for (_, h), new in zip(parts, news):
            for u in range(count):
                put(h, x0 + u, new[u], last)

    def e_rows(step, x0, count, ahead):
        last = step == STEPS - 1
        news = []
        for e, h in parts:
            es = [e_new(e, h, x0 + u, last) for u in range(count)]
            hs = [h_new(e, h, x0 + count + u) for u in range(count)] if ahead else []
            for u in range(count):
                put(e, x0 + u, es[u], last)
            for u in range(len(hs)):
                put(h, x0 + count + u, hs[u], last)
            news.append(es)
        for u in range(count):
            term = sum(news[0][u][n][0:cells] * news[1][u][n][0:cells] for n in range(3))
            total[x0 + u] = term if step == 0 else total[x0 + u] + term

    for step in range(STEPS):
        last = step == STEPS - 1
        pairs = (wide - 2 - 2 * step) // 2
        h_rows(step, 1, False)
        h_rows(step + 1, 2, last)

        def two_rows(i, _):
            e_rows(step, step + 1 + 2 * i, 2, True)
            return 0

        lax.fori_loop(0, pairs - 1, two_rows, 0, unroll=UNROLL)
        e_rows(step, step + 1 + 2 * (pairs - 1), 2, False)

    group = lax.broadcasted_iota(jnp.int32, (8, 128), 1) // DZ
    for line in range(cells * 2 // 8):
        packed = jnp.zeros((8, 128), jnp.float32)
        for n in range(8):
            x, half = HALO + (8 * line + n) // 2, n % 2
            moved = pltpu.roll(total[x, 8 * half:8 * half + 8, :], lax.rem(128 - start + DZ * n, 128), 1)
            packed = jnp.where(group == n, moved, packed)
        for peer in range(send.shape[0]):
            send[peer, 8 * line:8 * line + 8, :] = packed


def all_steps(cols, rows, waves, first_z, spread, state, halos):
    wide = state[0].shape[1]
    cells = wide - 2 * HALO
    out = pltpu.VMEM((3, cells, cells, 128), jnp.float32)
    plane = jax.ShapeDtypeStruct((wide, wide, 128), jnp.float32)
    return pl.pallas_call(
        functools.partial(steps_kernel, cols, rows),
        out_shape=(out, out, out, out,
                   jax.ShapeDtypeStruct((waves, cells * 2, 128), jnp.float32),
                   jax.ShapeDtypeStruct((12, wide, wide, 128), jnp.float32),
                   plane, plane, plane, plane),
        in_specs=[SMEM] + [VMEM] * 8,
        out_specs=[VMEM] * 10,
        scratch_shapes=[
            pltpu.VMEM((wide, cells, 128), jnp.float32),
            pltpu.VMEM((2, wide, 8, 128), jnp.float32),
        ],
        input_output_aliases={2: 5, 3: 6, 4: 7, 5: 8, 6: 9},
        compiler_params=pltpu.CompilerParams(vmem_limit_bytes=16 * 2**20),
        name="steps",
    )(first_z, spread, *state, *halos)[:5]


def gradient_kernel(parts, out):
    waves, lines, _ = parts.shape
    whole = parts[0]
    for wave in range(1, waves):
        whole = whole + parts[wave]
    for line in range(lines // 8):
        for n in range(8):
            x, half = (8 * line + n) // 2, n % 2
            block = whole[8 * line:8 * line + 8, :]
            if n:
                block = pltpu.roll(block, 128 - DZ * n, 1)
            out[x, 8 * half:8 * half + 8, :] = block[:, 0:DZ]


def gradient_of(parts):
    cells = parts.shape[1] // 2
    return pl.pallas_call(
        gradient_kernel,
        out_shape=jax.ShapeDtypeStruct((cells, cells, DZ), jnp.float32),
        in_specs=[VMEM],
        out_specs=VMEM,
        compiler_params=pltpu.CompilerParams(vmem_limit_bytes=8 * 2**20),
        name="gradient",
    )(parts)


def per_device(
    e_forward, h_forward, e_adjoint, h_adjoint, eps_table, material, pml_depth, design_start
):
    cols = TILE_COLS
    count = lax.axis_size("tile")
    rows = count // cols
    fields = (e_forward[0], h_forward[0], e_adjoint[0], h_adjoint[0])

    def swap(value, along_x, odd):
        return lax.ppermute(value, "tile", swap_pairs(count, cols, along_x, odd))

    xa, xb = edges(cols, fields, material, pml_depth)
    ra = swap(xa, True, 0)
    rb = swap(xb, True, 1)
    *state, ya, yb, spread = load(cols, eps_table, fields, material, pml_depth, xa)
    ryb = swap(yb, False, 1)
    rya = swap(ya, False, 0)
    ca, cb = corners(cols, ra, rb)
    rcb = swap(cb, False, 1)
    rca = swap(ca, False, 0)
    state = prepare(cols, rows, spread, state, ra, rb, ryb, rya)
    *outs, send = all_steps(cols, rows, lax.axis_size("wave"), design_start, spread, state,
                            (rcb, rca))
    parts = lax.all_to_all(send, "wave", 0, 0)
    gradient = gradient_of(parts)
    return tuple(out[None] for out in outs) + (gradient,)


def solution(mesh):
    return jax.shard_map(
        per_device,
        mesh=mesh,
        in_specs=(
            P("wave", None, "tile", None, None),
            P("wave", None, "tile", None, None),
            P("wave", None, "tile", None, None),
            P("wave", None, "tile", None, None),
            P("wave", None),
            P("tile", None, None),
            P("tile", None, None),
            P("tile"),
        ),
        out_specs=(
            P("wave", None, "tile", None, None),
            P("wave", None, "tile", None, None),
            P("wave", None, "tile", None, None),
            P("wave", None, "tile", None, None),
            P("tile", None, None),
        ),
        check_vma=False,
    )
```

```python
import functools

import jax
import jax.numpy as jnp
from jax import lax
from jax.experimental import pallas as pl
from jax.experimental.pallas import tpu as pltpu
from jax.sharding import PartitionSpec as P

STEPS = 4
DZ = 16
TILE_COLS = 8
HALO = STEPS
KINDS = 14
UNROLL = 4
CORNER_FLOPS = 2**36
LOAD_FLOPS = 2**30
PREPARE_FLOPS = 2**36

dt_step = 0.5
depth_scale = 4.0

VMEM = pl.BlockSpec(memory_space=pltpu.VMEM)
SMEM = pl.BlockSpec(memory_space=pltpu.SMEM)
HBM = pl.BlockSpec(memory_space=pltpu.HBM)
ANY = pl.BlockSpec(memory_space=pl.ANY)


def swap_pairs(count, cols, along_x, odd):
    rows = count // cols
    pairs = []
    for row in range(rows):
        for col in range(cols):
            place, size = (row, rows) if along_x else (col, cols)
            other = place + 1 if place % 2 == odd else place - 1
            if 0 <= other < size:
                target = other * cols + col if along_x else row * cols + other
                pairs.append((row * cols + col, target))
    return pairs


def low_half(shape):
    return lax.broadcasted_iota(jnp.int32, shape, len(shape) - 2) < 4


DEEP = (0, 1, 2, 4, 5, 6, 7, 8, 10, 11, 13)
SHALLOW = (3, 9, 12)
LAYERS = 4 * len(DEEP) + 3 * len(SHALLOW)


def layer_places():
    places = [(k, 4 * n, 4) for n, k in enumerate(DEEP)]
    return places + [(k, 4 * len(DEEP) + 3 * n, 3) for n, k in enumerate(SHALLOW)]


def tile_place(cols):
    me = lax.axis_index("tile")
    return lax.div(me, cols), lax.rem(me, cols)


def is_even(place):
    return lax.rem(place, 2) == 0


def edges_kernel(cols, ef, hf, ea, ha, kind, depth, xa, xb, whole, sems):
    row, _ = tile_place(cols)
    cells = kind.shape[0]
    sources = [(ef, hf, ea, ha)[k // 3].at[k % 3] for k in range(12)] + [kind, depth]
    loads = []
    for side, to in enumerate((xa, xb)):
        at_end = is_even(row) if side == 0 else jnp.logical_not(is_even(row))
        for k, place, count in layer_places():
            at = jnp.where(at_end, cells - count, 0)
            target = to.at[pl.ds(place, count)]
            if k >= 12:
                target = whole.at[2 * side + k - 12, pl.ds(0, count)]
            loads.append(pltpu.make_async_copy(
                sources[k].at[pl.ds(at, count)], target, sems.at[side * KINDS + k]))
            loads[-1].start()
    for load in loads:
        load.wait()
    for side, to in enumerate((xa, xb)):
        for k, place, count in layer_places():
            if k >= 12:
                to[place:place + count] = whole[2 * side + k - 12, 0:count].astype(jnp.float32)


def in_hbm(values):
    return [pltpu.with_memory_space_constraint(value, pltpu.HBM) for value in values]


def edges(cols, fields, kind, depth):
    cells = kind.shape[0]
    layers = jax.ShapeDtypeStruct((LAYERS, cells, 128), jnp.float32)
    return pl.pallas_call(
        functools.partial(edges_kernel, cols),
        out_shape=(layers, layers),
        in_specs=[HBM] * 6,
        out_specs=[VMEM] * 2,
        scratch_shapes=[
            pltpu.VMEM((4, HALO, cells, 128), jnp.int32),
            pltpu.SemaphoreType.DMA((2 * KINDS,)),
        ],
        compiler_params=pltpu.CompilerParams(vmem_limit_bytes=16 * 2**20),
        cost_estimate=pl.CostEstimate(flops=2**20, bytes_accessed=2**20, transcendentals=0),
        name="edges",
    )(*in_hbm((*fields, kind, depth)))


def load_kernel(cols, eps_table, ef, hf, ea, ha, kind, depth, after,
                field, ca, cb, da, db, ya, yb, spread, whole, few, sems):
    _, col = tile_place(cols)
    cells = kind.shape[0]
    own = pl.ds(HALO, cells)
    loads = []
    for n, k in enumerate((12, 13) + tuple(range(12))):
        source = (kind, depth)[k - 12] if k >= 12 else (ef, hf, ea, ha)[k // 3].at[k % 3]
        target = whole.at[k - 12] if k >= 12 else field.at[k, own, pl.ds(0, cells), :]
        loads.append(pltpu.make_async_copy(source, target, sems.at[k]))
        loads[-1].start()
    loads.append(pltpu.make_async_copy(eps_table, few, sems.at[KINDS]))
    loads[-1].start()
    for n in (0, 1, -1):
        loads[n].wait()
    table = [few[0, m] for m in range(spread.shape[0])]
    for m, eps in enumerate(table):
        spread[m] = jnp.full(spread.shape[1:], eps, jnp.float32)

    def fill(x, _):
        values = coefficients(whole[0, x].astype(jnp.float32), whole[1, x].astype(jnp.float32),
                              table, None)
        for plane, value in zip((ca, cb, da, db), values):
            plane[HALO + x, 0:cells, :] = value
        return 0

    lax.fori_loop(0, cells, fill, 0, unroll=4)
    for load in loads[2:-1]:
        load.wait()

    def strips(to_a, to_b):
        for k in range(KINDS):
            for out, ys in ((ya, to_a), (yb, to_b)):
                strip = (whole[k - 12, :, ys, :].astype(jnp.float32) if k >= 12
                         else field[k, own, ys, :])
                out[k * cells:(k + 1) * cells] = strip

    @pl.when(is_even(col))
    def _():
        strips(slice(12, 16), slice(0, 4))

    @pl.when(jnp.logical_not(is_even(col)))
    def _():
        strips(slice(0, 4), slice(12, 16))


def load(cols, eps_table, fields, kind, depth, after):
    cells = kind.shape[0]
    wide = cells + 2 * HALO
    plane = jax.ShapeDtypeStruct((wide, wide, 128), jnp.float32)
    return pl.pallas_call(
        functools.partial(load_kernel, cols),
        out_shape=(jax.ShapeDtypeStruct((12, wide, wide, 128), jnp.float32),
                   plane, plane, plane, plane,
                   jax.ShapeDtypeStruct((KINDS * cells, 4, 128), jnp.float32),
                   jax.ShapeDtypeStruct((KINDS * cells, 4, 128), jnp.float32),
                   jax.ShapeDtypeStruct((eps_table.shape[1], 8, 128), jnp.float32)),
        in_specs=[HBM] * 7 + [ANY],
        out_specs=[VMEM] * 8,
        scratch_shapes=[
            pltpu.VMEM((2, cells, cells, 128), jnp.int32),
            pltpu.SMEM(eps_table.shape, jnp.float32),
            pltpu.SemaphoreType.DMA((KINDS + 1,)),
        ],
        compiler_params=pltpu.CompilerParams(vmem_limit_bytes=16 * 2**20),
        cost_estimate=pl.CostEstimate(flops=LOAD_FLOPS, bytes_accessed=2**22, transcendentals=0),
        name="load",
    )(*in_hbm((eps_table, *fields, kind, depth)), after)


def corner_kernel(cols, ra, rb, ca, cb):
    _, col = tile_place(cols)

    def put(to_a, to_b):
        for n, source in enumerate((ra, rb)):
            cb[n * LAYERS:(n + 1) * LAYERS] = source[:, to_b, :]
            ca[n * LAYERS:(n + 1) * LAYERS] = source[:, to_a, :]

    @pl.when(is_even(col))
    def _():
        put(slice(12, 16), slice(0, 4))

    @pl.when(jnp.logical_not(is_even(col)))
    def _():
        put(slice(0, 4), slice(12, 16))


def corners(cols, ra, rb):
    corner = jax.ShapeDtypeStruct((2 * LAYERS, HALO, 128), jnp.float32)
    return pl.pallas_call(
        functools.partial(corner_kernel, cols),
        out_shape=(corner, corner),
        in_specs=[VMEM] * 2,
        out_specs=[VMEM] * 2,
        compiler_params=pltpu.CompilerParams(vmem_limit_bytes=16 * 2**20),
        cost_estimate=pl.CostEstimate(flops=CORNER_FLOPS, bytes_accessed=2**20, transcendentals=0),
        name="corners",
    )(ra, rb)


def coefficients(m, d, table, outside):
    eps = jnp.where(m < 0.5, table[0],
                    jnp.where(m < 1.5, table[1], jnp.where(m < 2.5, table[2], table[3])))
    ramp = d / depth_scale
    sigma = ramp * ramp
    s_e = sigma * dt_step / (2.0 * eps)
    s_h = sigma * dt_step / 2.0
    values = ((1.0 - s_e) / (1.0 + s_e), dt_step / (eps * (1.0 + s_e)),
              (1.0 - s_h) / (1.0 + s_h), dt_step / (1.0 + s_h))
    if outside is None:
        return values
    return (values[0], jnp.where(outside, 0.0, values[1]),
            values[2], jnp.where(outside, 0.0, values[3]))


def spread_table(spread):
    return [spread[m, 0:1, :] for m in range(spread.shape[0])]


def outside_rows(x, cells, row, rows):
    return jnp.logical_or(jnp.logical_and(x < HALO, row == 0),
                          jnp.logical_and(x >= HALO + cells, row == rows - 1))


def halo_places(row, cells):
    even = is_even(row)
    after, before = HALO + cells, 0
    deep = jnp.where(even, after, before), jnp.where(even, before, after)
    shallow = jnp.where(even, after, before + 1), jnp.where(even, before + 1, after)
    return deep, shallow


def sides(col, put):
    @pl.when(is_even(col))
    def _():
        put(0, HALO)

    @pl.when(jnp.logical_not(is_even(col)))
    def _():
        put(HALO, 0)


def fill_columns(cols, table, matter, planes, row_of, count, outside):
    _, col = tile_place(cols)
    cells = planes[0].shape[0] - 2 * HALO
    after = low_half((8, 128))
    outside_y = jnp.logical_or(jnp.logical_and(after, col == cols - 1),
                               jnp.logical_and(jnp.logical_not(after), col == 0))

    def fill(n, _):
        x = row_of(n)
        values = coefficients(matter[0, x], matter[1, x], table,
                              jnp.logical_or(outside_y, outside(x)) if outside else outside_y)
        for plane, value in zip(planes, values):
            plane[x, cells:cells + 8, :] = value
        return 0

    lax.fori_loop(0, count, fill, 0, unroll=4)


def rim_row(cells):
    return lambda n: jnp.where(n < HALO, n, n + cells)


def prepare_kernel(cols, rows, spread, field_in, ca_in, cb_in, da_in, db_in, ra, rb, ryb, rya,
                   field, ca, cb, da, db, matter, strip):
    row, col = tile_place(cols)
    cells = ra.shape[1]
    own = slice(HALO, HALO + cells)

    def columns(first_a, first_b):
        for k in range(KINDS):
            to, base = (field.at[k], cells) if k < 12 else (strip.at[k - 12], 0)
            to[own, base + first_a:base + first_a + 4, :] = rya[k * cells:(k + 1) * cells]
            to[own, base + first_b:base + first_b + 4, :] = ryb[k * cells:(k + 1) * cells]

    sides(col, columns)
    fill_columns(cols, spread_table(spread), strip, (ca, cb, da, db), lambda n: n + HALO, cells,
                 None)
    table = spread_table(spread)
    deep, shallow = halo_places(row, cells)
    for k, place, count in layer_places():
        for side, layers in enumerate((ra, rb)):
            here = pl.ds((deep if count == HALO else shallow)[side], count)
            to = field.at[k] if k < 12 else matter.at[k - 12]
            to[here, 0:cells, :] = layers[place:place + count]

    def fill(n, _):
        x = rim_row(cells)(n)
        values = coefficients(matter[0, x], matter[1, x], table,
                              outside_rows(x, cells, row, rows))
        for plane, value in zip((ca, cb, da, db), values):
            plane[x, 0:cells, :] = value
        return 0

    lax.fori_loop(0, 2 * HALO, fill, 0, unroll=4)


def prepare(cols, rows, spread, state, ra, rb, ryb, rya):
    cells = ra.shape[1]
    wide = cells + 2 * HALO
    return pl.pallas_call(
        functools.partial(prepare_kernel, cols, rows),
        out_shape=tuple(jax.ShapeDtypeStruct(part.shape, part.dtype) for part in state),
        in_specs=[VMEM] * 10,
        out_specs=[VMEM] * 5,
        scratch_shapes=[pltpu.VMEM((2, wide, cells, 128), jnp.float32),
                        pltpu.VMEM((2, wide, 8, 128), jnp.float32)],
        input_output_aliases={n + 1: n for n in range(5)},
        compiler_params=pltpu.CompilerParams(vmem_limit_bytes=16 * 2**20),
        cost_estimate=pl.CostEstimate(flops=PREPARE_FLOPS, bytes_accessed=2**22, transcendentals=0),
        name="prepare",
    )(spread, *state, ra, rb, ryb, rya)


def steps_kernel(cols, rows, first_z, spread, field_in, ca_in, cb_in, da_in, db_in, rcb, rca,
                 ef_out, hf_out, ea_out, ha_out, send, field, ca, cb, da, db, total, matter):
    start = first_z[0]
    table = spread_table(spread)
    row, col = tile_place(cols)
    wide = ca.shape[0]
    cells = wide - 2 * HALO
    deep, shallow = halo_places(row, cells)

    def columns(first_a, first_b):
        for k, place, count in layer_places():
            to, base = (field.at[k], cells) if k < 12 else (matter.at[k - 12], 0)
            for side in range(2):
                here = pl.ds((deep if count == HALO else shallow)[side], count)
                at = side * LAYERS + place
                to[here, base + first_a:base + first_a + 4, :] = rca[at:at + count]
                to[here, base + first_b:base + first_b + 4, :] = rcb[at:at + count]

    sides(col, columns)
    fill_columns(cols, table, matter, (ca, cb, da, db), rim_row(cells), 2 * HALO,
                 lambda x: outside_rows(x, cells, row, rows))

    lane = lax.broadcasted_iota(jnp.int32, (wide, 128), 1)
    top_z, bottom_z = lane == 127, lane == 0

    def up_z(v):
        return jnp.where(top_z, 0.0, pltpu.roll(v, 127, 1))

    def down_z(v):
        return jnp.where(bottom_z[0:v.shape[0]], 0.0, pltpu.roll(v, 1, 1))

    def up_y(v):
        return pltpu.roll(v, wide - 1, 0)

    def down_y(v):
        return pltpu.roll(v, 1, 0)

    parts = ((0, 3), (6, 9))
    outs = {0: ef_out, 3: hf_out, 6: ea_out, 9: ha_out}

    def h_new(e, h, x):
        dax, dbx = da[x], db[x]
        ex, ey, ez = field[e, x], field[e + 1, x], field[e + 2, x]
        ey1, ez1 = field[e + 1, x + 1], field[e + 2, x + 1]
        return (dax * field[h, x] - dbx * ((up_y(ez) - ez) - (up_z(ey) - ey)),
                dax * field[h + 1, x] - dbx * ((up_z(ex) - ex) - (ez1 - ez)),
                dax * field[h + 2, x] - dbx * ((ey1 - ey) - (up_y(ex) - ex)))

    def e_new(e, h, x, last):
        ys = cells if last else wide
        cax, cbx = ca[x, 0:ys], cb[x, 0:ys]
        all_hx, hy, all_hz = field[h, x], field[h + 1, x, 0:ys], field[h + 2, x]
        hx, hz = all_hx[0:ys], all_hz[0:ys]
        hy1, hz1 = field[h + 1, x - 1, 0:ys], field[h + 2, x - 1, 0:ys]
        return (cax * field[e, x, 0:ys] + cbx * ((hz - down_y(all_hz)[0:ys]) - (hy - down_z(hy))),
                cax * field[e + 1, x, 0:ys] + cbx * ((hx - down_z(hx)) - (hz - hz1)),
                cax * field[e + 2, x, 0:ys] + cbx * ((hy - hy1) - (hx - down_y(all_hx)[0:ys])))

    def put(k, x, new, last):
        for n in range(3):
            if last:
                outs[k][n, x - HALO] = new[n][0:cells]
            if not last or (k in (3, 9)):
                field[k + n, x] = new[n]

    def before_first(x):
        for e, h in parts:
            new = h_new(e, h, x)
            for n in (1, 2):
                field[h + n, x] = new[n]

    def h_rows(x0, count, last):
        news = [[h_new(e, h, x0 + u) for u in range(count)] for e, h in parts]
        for (_, h), new in zip(parts, news):
            for u in range(count):
                put(h, x0 + u, new[u], last)

    def e_rows(step, x0, count, ahead):
        last = step == STEPS - 1
        news = []
        for e, h in parts:
            es = [e_new(e, h, x0 + u, last) for u in range(count)]
            hs = [h_new(e, h, x0 + count + u) for u in range(count)] if ahead else []
            for u in range(count):
                put(e, x0 + u, es[u], last)
            for u in range(len(hs)):
                put(h, x0 + count + u, hs[u], last)
            news.append(es)
        for u in range(count):
            term = sum(news[0][u][n][0:cells] * news[1][u][n][0:cells] for n in range(3))
            total[x0 + u] = term if step == 0 else total[x0 + u] + term

    for step in range(STEPS):
        last = step == STEPS - 1
        pairs = (wide - 2 - 2 * step) // 2
        before_first(step)
        h_rows(step + 1, 2, last)

        def two_rows(i, _):
            e_rows(step, step + 1 + 2 * i, 2, True)
            return 0

        lax.fori_loop(0, pairs - 1, two_rows, 0, unroll=UNROLL)
        e_rows(step, step + 1 + 2 * (pairs - 1), 2, False)

    group = lax.broadcasted_iota(jnp.int32, (8, 128), 1) // DZ
    for line in range(cells * 2 // 8):
        packed = jnp.zeros((8, 128), jnp.float32)
        for n in range(8):
            x, half = HALO + (8 * line + n) // 2, n % 2
            moved = pltpu.roll(total[x, 8 * half:8 * half + 8, :], lax.rem(128 - start + DZ * n, 128), 1)
            packed = jnp.where(group == n, moved, packed)
        for peer in range(send.shape[0]):
            send[peer, 8 * line:8 * line + 8, :] = packed


def all_steps(cols, rows, waves, first_z, spread, state, halos):
    wide = state[0].shape[1]
    cells = wide - 2 * HALO
    out = pltpu.VMEM((3, cells, cells, 128), jnp.float32)
    plane = jax.ShapeDtypeStruct((wide, wide, 128), jnp.float32)
    return pl.pallas_call(
        functools.partial(steps_kernel, cols, rows),
        out_shape=(out, out, out, out,
                   jax.ShapeDtypeStruct((waves, cells * 2, 128), jnp.float32),
                   jax.ShapeDtypeStruct((12, wide, wide, 128), jnp.float32),
                   plane, plane, plane, plane),
        in_specs=[SMEM] + [VMEM] * 8,
        out_specs=[VMEM] * 10,
        scratch_shapes=[
            pltpu.VMEM((wide, cells, 128), jnp.float32),
            pltpu.VMEM((2, wide, 8, 128), jnp.float32),
        ],
        input_output_aliases={2: 5, 3: 6, 4: 7, 5: 8, 6: 9},
        compiler_params=pltpu.CompilerParams(vmem_limit_bytes=16 * 2**20),
        name="steps",
    )(first_z, spread, *state, *halos)[:5]


def gradient_kernel(parts, out):
    waves, lines, _ = parts.shape
    whole = parts[0]
    for wave in range(1, waves):
        whole = whole + parts[wave]
    for line in range(lines // 8):
        for n in range(8):
            x, half = (8 * line + n) // 2, n % 2
            block = whole[8 * line:8 * line + 8, :]
            if n:
                block = pltpu.roll(block, 128 - DZ * n, 1)
            out[x, 8 * half:8 * half + 8, :] = block[:, 0:DZ]


def gradient_of(parts):
    cells = parts.shape[1] // 2
    return pl.pallas_call(
        gradient_kernel,
        out_shape=jax.ShapeDtypeStruct((cells, cells, DZ), jnp.float32),
        in_specs=[VMEM],
        out_specs=VMEM,
        compiler_params=pltpu.CompilerParams(vmem_limit_bytes=8 * 2**20),
        name="gradient",
    )(parts)


def per_device(
    e_forward, h_forward, e_adjoint, h_adjoint, eps_table, material, pml_depth, design_start
):
    cols = TILE_COLS
    count = lax.axis_size("tile")
    rows = count // cols
    fields = (e_forward[0], h_forward[0], e_adjoint[0], h_adjoint[0])

    def swap(value, along_x, odd):
        return lax.ppermute(value, "tile", swap_pairs(count, cols, along_x, odd))

    xa, xb = edges(cols, fields, material, pml_depth)
    ra = swap(xa, True, 0)
    rb = swap(xb, True, 1)
    *state, ya, yb, spread = load(cols, eps_table, fields, material, pml_depth, xa)
    ryb = swap(yb, False, 1)
    rya = swap(ya, False, 0)
    ca, cb = corners(cols, ra, rb)
    rcb = swap(cb, False, 1)
    rca = swap(ca, False, 0)
    state = prepare(cols, rows, spread, state, ra, rb, ryb, rya)
    *outs, send = all_steps(cols, rows, lax.axis_size("wave"), design_start, spread, state,
                            (rcb, rca))
    parts = lax.all_to_all(send, "wave", 0, 0)
    gradient = gradient_of(parts)
    return tuple(out[None] for out in outs) + (gradient,)


def solution(mesh):
    return jax.shard_map(
        per_device,
        mesh=mesh,
        in_specs=(
            P("wave", None, "tile", None, None),
            P("wave", None, "tile", None, None),
            P("wave", None, "tile", None, None),
            P("wave", None, "tile", None, None),
            P("wave", None),
            P("tile", None, None),
            P("tile", None, None),
            P("tile"),
        ),
        out_specs=(
            P("wave", None, "tile", None, None),
            P("wave", None, "tile", None, None),
            P("wave", None, "tile", None, None),
            P("wave", None, "tile", None, None),
            P("tile", None, None),
        ),
        check_vma=False,
    )
```
